32 devices in a mesh: dp: 2 (over x), row: 4 (over z), col: 4 (over y, core).
Axes of the slice: x: 2, y: 2, z: 4, core: 2. Of those that a mesh axis runs over, the one named last changes fastest.
Arguments:
- block_input: bfloat16 [32768, 896], P(('dp', 'row', 'col')), may hold values from -6 to 6
- first_gain: bfloat16 [896], P('col'), may hold values from 0.5 to 1.5
- joint_weight: bfloat16 [896, 1152], P('row', 'col'), may hold values from -0.1875 to 0.1875
- joint_bias: bfloat16 [1152], P('col'), may hold values from -3 to 3
- output_weight: bfloat16 [896, 896], P('row', 'col'), may hold values from -1 to 1
- second_gain: bfloat16 [896], P('col'), may hold values from 0.5 to 1.5
- gate_weight: bfloat16 [896, 4864], P('row', 'col'), may hold values from -0.1875 to 0.1875
- up_weight: bfloat16 [896, 4864], P('row', 'col'), may hold values from -0.1875 to 0.1875
- down_weight: bfloat16 [4864, 896], P('col', 'row'), may hold values from -0.078125 to 0.078125
- cotangent: bfloat16 [32768, 896], P(('dp', 'row', 'col')), may hold values from -6 to 6
Outputs:
- block_output: bfloat16 [32768, 896], P(('dp', 'row', 'col'))
- input_grad: bfloat16 [32768, 896], P(('dp', 'row', 'col'))
- first_gain_grad: float32 [896], P('col')
- joint_weight_grad: float32 [896, 1152], P('row', 'col')
- query_key_bias_grad: float32 [1024], P('col')
- value_bias_grad: float32 [128], P('col')
- output_weight_grad: float32 [896, 896], P('row', 'col')
- second_gain_grad: float32 [896], P('col')
- gate_weight_grad: float32 [896, 4864], P('row', 'col')
- up_weight_grad: float32 [896, 4864], P('row', 'col')
- down_weight_grad: float32 [4864, 896], P('col', 'row')
The draws below stay inside these ranges and needn't reach their ends.
All inputs are finite; a program needn't handle non-finite values.
Results may differ from the reference program's by a relative error of at most 0.018.
Values may be sent and summed in bfloat16 or wider, within the bound.
No kernel may reach another device: no remote copies, remote signals or barrier semaphores. Data moves between devices by JAX's collectives and lax.ppermute only.
A program may use at most 256 MiB of HBM per device.

```python
import math
import jax
import jax.numpy as jnp
from jax import lax

D = 896
FF = 4864
QH = 14
KVH = 2
HD = 64
SEQ_LEN = 1024
QKV = 1152
QK = 1024
TOKENS = 32768


def block_scale(rng, dims, pieces, smallest, top_value):
    factor_of, own = 1.0, jax.random.fold_in(rng, 6)
    for axis_at, shards_of in pieces:
        draws = jnp.exp(jax.random.uniform(jax.random.fold_in(own, axis_at), (shards_of,), jnp.float32, smallest / len(pieces), top_value / len(pieces)))
        factor_of = factor_of * jnp.repeat(draws, dims[axis_at] // shards_of).reshape([-1 if axis == axis_at else 1 for axis in range(len(dims))])
    return factor_of


def noise(stream_key, extent, scale, limit, cuts=(), held_as=jnp.bfloat16):
    factor_of = block_scale(stream_key, extent, cuts, -0.22, 0.18) if cuts else 1.0
    values = jax.random.normal(stream_key, extent, jnp.float32) * scale * factor_of
    return jnp.minimum(jnp.maximum(values, -limit), limit).astype(held_as)


def setup_inputs(seed: int = 0) -> dict:
    seeds = jax.random.split(jax.random.key(seed), 11)
    block_input = noise(seeds[0], (TOKENS, D), 1.0, 6.0, ((0, 32),))
    first_gain = jnp.clip(1.0 + 0.1 * jax.random.normal(seeds[1], (D,), jnp.float32), 0.5, 1.5).astype(jnp.bfloat16)
    joint_weight = noise(seeds[2], (D, QKV), D ** -0.5, 0.1875, ((0, 4), (1, 4)))
    joint_bias = noise(seeds[3], (QKV,), 0.5, 3.0, ((0, 4),))
    output_weight = noise(seeds[4], (D, D), (D // 32) ** -0.5, 1.0, ((0, 4), (1, 4)))
    second_gain = jnp.clip(1.0 + 0.1 * jax.random.normal(seeds[5], (D,), jnp.float32), 0.5, 1.5).astype(jnp.bfloat16)
    gate_weight = noise(seeds[6], (D, FF), D ** -0.5, 0.1875, ((0, 4), (1, 4)))
    up_weight = noise(seeds[7], (D, FF), D ** -0.5, 0.1875, ((0, 4), (1, 4)))
    down_weight = noise(seeds[8], (FF, D), FF ** -0.5, 0.078125, ((0, 4), (1, 4)))
    cotangent = noise(seeds[9], (TOKENS, D), 1.0, 6.0, ((0, 32),))
    return dict(block_input=block_input, first_gain=first_gain, joint_weight=joint_weight, joint_bias=joint_bias, output_weight=output_weight, second_gain=second_gain, gate_weight=gate_weight, up_weight=up_weight, down_weight=down_weight, cotangent=cotangent)


EPS = 1e-06
BASE = 1000000.0
MASKED = -1e+30
HIGH = lax.Precision.HIGHEST

@jax.custom_vjp
def low(v):
    return lax.optimization_barrier(v.astype(jnp.bfloat16)).astype(jnp.float32)

@jax.custom_vjp
def low_back(v):
    return v

def low_keep(v):
    return (low(v), None)

def low_pass(kept, grad):
    return (grad,)

def back_keep(v):
    return (v, None)

def back_low(kept, grad):
    return (low(grad),)
low.defvjp(low_keep, low_pass)
low_back.defvjp(back_keep, back_low)

def rotary_tables(length, head):
    half = head // 2
    freq = BASE ** (-(jnp.arange(half, dtype=jnp.float32) * 2.0 / head))
    angle = jnp.arange(length, dtype=jnp.float32)[:, None] * freq[None, :]
    return (jnp.cos(angle)[None, :, None, :], jnp.sin(angle)[None, :, None, :])

def rotate(values, cosine, sine):
    half = values.shape[-1] // 2
    first = values[..., :half]
    second = values[..., half:]
    return jnp.concatenate([first * cosine - second * sine, second * cosine + first * sine], -1)

def normalize(values, gain):
    return values * lax.rsqrt(lax.optimization_barrier(jnp.mean(values * values, -1, keepdims=True)) + EPS) * gain

def matmul(left, right):
    return jnp.dot(left, right, precision=HIGH, preferred_element_type=jnp.float32)

def attend_block(query_block, key_rows, value_rows, positions):
    scale = query_block.shape[-1] ** (-0.5)
    scores = jnp.einsum('qkgd,lkd->kgql', query_block, key_rows, precision=HIGH) * scale
    scores = low_back(scores)
    allowed = positions[:, None] >= jnp.arange(key_rows.shape[0])[None, :]
    scores = jnp.where(allowed[None, None], scores, MASKED)
    peak = lax.optimization_barrier(jnp.max(scores, -1, keepdims=True))
    weights = jnp.exp(scores - peak)
    prob = weights / lax.optimization_barrier(jnp.sum(weights, -1, keepdims=True))
    return jnp.einsum('kgql,lkd->qkgd', low(prob), value_rows, precision=HIGH)

def attend(queries, key_rows, value_rows):
    length = queries.shape[0]
    rows = min(512, length)
    blocks = length // rows
    query_blocks = queries.reshape(blocks, rows, KVH, QH // KVH, HD)
    positions = jnp.arange(length).reshape(blocks, rows)

    def one_block(item):
        return attend_block(item[0], key_rows, value_rows, item[1])
    return lax.map(jax.checkpoint(one_block), (query_blocks, positions)).reshape(length, QH * HD)

def layer(inputs, params):
    first_gain, joint_weight, joint_bias, output_weight, second_gain, gate_weight, up_weight, down_weight = params
    seqs = inputs.shape[0]
    width = QH * HD
    kv_width = KVH * HD
    rows = inputs.reshape(-1, D)
    first_act = low(normalize(rows, first_gain))
    joint = low_back(matmul(first_act, joint_weight) + joint_bias)
    cosine, sine = rotary_tables(SEQ_LEN, HD)
    queries = low(rotate(joint[:, :width].reshape(seqs, SEQ_LEN, QH, HD), cosine, sine))
    key_rows = low(rotate(joint[:, width:width + kv_width].reshape(seqs, SEQ_LEN, KVH, HD), cosine, sine))
    value_rows = low(joint[:, width + kv_width:].reshape(seqs, SEQ_LEN, KVH, HD))

    def one_sequence(item):
        return attend(item[0], item[1], item[2])
    attended = lax.map(one_sequence, (queries, key_rows, value_rows))
    attended = low(low_back(attended.reshape(-1, width)))
    resid = rows + low_back(matmul(attended, output_weight))
    second_act = low(normalize(resid, second_gain))
    gate = low_back(matmul(second_act, gate_weight))
    up_part = low_back(matmul(second_act, up_weight))
    hidden = low(jax.nn.silu(gate) * up_part)
    return (resid + matmul(hidden, down_weight)).reshape(inputs.shape)

def reference(block_input, first_gain, joint_weight, joint_bias, output_weight, second_gain, gate_weight, up_weight, down_weight, cotangent):
    params = tuple((p.astype(jnp.float32) for p in (first_gain, joint_weight, joint_bias, output_weight, second_gain, gate_weight, up_weight, down_weight)))
    seq_total = TOKENS // SEQ_LEN
    group = math.gcd(seq_total, max(1, 4096 // SEQ_LEN))
    inputs = block_input.astype(jnp.float32).reshape(seq_total // group, group, SEQ_LEN, D)
    upstream = cotangent.astype(jnp.float32).reshape(seq_total // group, group, SEQ_LEN, D)

    def step(totals, item):
        outputs, pull = jax.vjp(layer, item[0], params)
        input_part, param_parts = pull(item[1])
        totals = tuple((a + b for a, b in zip(totals, param_parts)))
        return (totals, (outputs.astype(jnp.bfloat16), input_part.astype(jnp.bfloat16)))
    zeros = tuple((jnp.zeros_like(p) for p in params))
    totals, results = lax.scan(step, zeros, (inputs, upstream))
    outputs = results[0].reshape(TOKENS, D)
    input_grad = results[1].reshape(TOKENS, D)
    bias_total = totals[2]
    return (outputs, input_grad, totals[0], totals[1], bias_total[:QK], bias_total[QK:], totals[3], totals[4], totals[5], totals[6], totals[7])
```

```python
import functools

import jax
import jax.numpy as jnp
from jax import lax
from jax.experimental import pallas as pl
from jax.experimental.pallas import tpu as pltpu
from jax.sharding import PartitionSpec as P

QH = 14
KVH = 2
HD = 64
SEQ_LEN = 1024
GROUP = QH // KVH
WIDTH = QH * HD
KV_WIDTH = KVH * HD
QK_WIDTH = WIDTH + KV_WIDTH
QKV = QK_WIDTH + KV_WIDTH

EPS = 1e-06
BASE = 1000000.0
MASKED = -1e30
LANES = 128
BLOCK = 256

NN = (((1,), (0,)), ((), ()))
NT = (((1,), (1,)), ((), ()))
TN = (((0,), (0,)), ((), ()))
VMEM_BYTES = 56 * 1024 * 1024


def dot(left, right, dims=NN):
    return lax.dot_general(left, right, dims, preferred_element_type=jnp.float32)


def low(values):
    return values.astype(jnp.bfloat16)


def add(left, right):
    return low(left.astype(jnp.float32) + right.astype(jnp.float32))


def cost(flops, moved, transcendentals=0):
    return pl.CostEstimate(
        flops=int(flops), bytes_accessed=int(moved), transcendentals=int(transcendentals)
    )


def flip(values, axis, size, bit):
    return lax.ppermute(values, axis, [(i, i ^ bit) for i in range(size)])


def shift(values, axis, size):
    return lax.ppermute(values, axis, [(i, (i + 1) % size) for i in range(size)])


def join(mine, other, odd, axis):
    first = jnp.where(odd, other, mine)
    second = jnp.where(odd, mine, other)
    return jnp.concatenate([first, second], axis)


def half_of(values, which, axis):
    size = values.shape[axis] // 2
    return lax.dynamic_slice_in_dim(values, which * size, size, axis)


def after(values, done):
    return lax.optimization_barrier((values, done))[0]


class Grid:
    def __init__(self, sizes):
        self.dp, self.row, self.col = sizes["dp"], sizes["row"], sizes["col"]
        self.at_dp = lax.axis_index("dp")
        self.at_row = lax.axis_index("row")
        self.at_col = lax.axis_index("col")
        self.odd_dp = self.at_dp % 2
        self.core = self.at_col % 2
        self.pair = self.at_col // 2

    def gather_rows(self, block, axis, holds=()):
        size = block.shape[axis]
        mine = half_of(block, self.odd_dp, axis)
        shape = list(block.shape)
        shape[axis] = size * self.row
        full = jnp.zeros(shape, block.dtype)
        full = lax.dynamic_update_slice_in_dim(full, block, self.at_row * size, axis)
        for step in range(1, self.row):
            mine = shift(mine, "row", self.row)
            if holds:
                mine = after(mine, holds[step - 1])
            other = flip(mine, "dp", self.dp, 1)
            if holds:
                other = after(other, holds[step])
            whole = join(mine, other, self.odd_dp == 1, axis)
            at = (self.at_row - step) % self.row
            full = lax.dynamic_update_slice_in_dim(full, whole, at * size, axis)
        return full, mine

    def gather_all(self, block):
        other = flip(block, "col", self.col, 2)
        both = join(block[None], other[None], self.pair == 1, 0)
        mine, last = self.gather_rows(both, 1)
        other = flip(mine, "col", self.col, 1)
        first = jnp.where(self.core == 1, other, mine)
        second = jnp.where(self.core == 1, mine, other)
        return [first[0], second[0], first[1], second[1]], last

    def gather_small(self, block):
        other = flip(block, "col", self.col, 2)
        both = join(block[None], other[None], self.pair == 1, 0)
        other = flip(both, "col", self.col, 1)
        both, other = both[:, None], other[:, None]
        whole = join(both, other, self.core == 1, 1)
        return whole.reshape((self.col,) + block.shape)

    def swap_halves(self, part):
        size = part.shape[0] // self.row
        blocks = part.reshape(self.row, size, part.shape[1])
        mine = half_of(blocks, self.odd_dp, 1)
        return mine, flip(half_of(blocks, 1 - self.odd_dp, 1), "dp", self.dp, 1)

    def scatter_half(self, mine, holds=()):
        def block_at(step):
            at = (self.at_row - step) % self.row
            return lax.dynamic_index_in_dim(mine, at, 0, False).astype(jnp.float32)

        total = low(block_at(1))
        for step in range(1, self.row):
            got = shift(total, "row", self.row)
            if holds:
                got = after(got, holds[step - 1])
            total = low(got.astype(jnp.float32) + block_at(step + 1))
        bit = 2
        while bit < self.dp:
            got = flip(total, "dp", self.dp, bit)
            total = low(total.astype(jnp.float32) + got.astype(jnp.float32))
            bit *= 2
        return total

    def both_halves(self, total):
        other = flip(total, "dp", self.dp, 1)
        return join(total, other, self.odd_dp == 1, 0)

    def scatter_all(self, pieces):
        evens = jnp.stack([pieces[0], pieces[2]])
        odds = jnp.stack([pieces[1], pieces[3]])
        mine = jnp.where(self.core == 1, odds, evens)
        theirs = jnp.where(self.core == 1, evens, odds)
        got = flip(theirs, "col", self.col, 1)
        mine = add(mine, got)
        got = flip(jnp.where(self.pair == 1, mine[0], mine[1]), "col", self.col, 2)
        mine = jnp.where(self.pair == 1, mine[1], mine[0])
        mine, got = self.swap_halves(add(mine, got))
        return self.both_halves(self.scatter_half(add(mine, got)))

    def sum_small(self, values):
        for axis, size in (("col", self.col), ("row", self.row), ("dp", self.dp)):
            bit = 1
            while bit < size:
                values = values + flip(values, axis, size, bit)
                bit *= 2
        return values


def turn_pairs(values, cosine, sine):
    lane = lax.broadcasted_iota(jnp.int32, values.shape, 1)
    before = pltpu.roll(values, HD // 2, 1)
    after = pltpu.roll(values, LANES - HD // 2, 1)
    partner = jnp.where(lane % HD < HD // 2, after, before)
    return values * cosine + partner * sine


def joint_kernel(x_ref, gain_ref, weight_ref, bias_ref, cos_ref, sin_ref, act_ref, out_ref):
    inputs = x_ref[...].astype(jnp.float32)
    inverse = lax.rsqrt(jnp.mean(inputs * inputs, -1, keepdims=True) + EPS)
    act = low(inputs * inverse * gain_ref[...])
    act_ref[...] = act
    joint = dot(act, weight_ref[...]) + bias_ref[...]
    cosine, sine = cos_ref[...], sin_ref[...]
    for start in range(0, QK_WIDTH, LANES):
        turned = turn_pairs(joint[:, start : start + LANES], cosine, sine)
        out_ref[:, start : start + LANES] = low(turned)
    out_ref[:, QK_WIDTH:] = low(joint[:, QK_WIDTH:])


def joint_projection(inputs, gain, weight, bias, cosine, sine):
    tokens, width = inputs.shape
    steps = SEQ_LEN // BLOCK
    return pl.pallas_call(
        joint_kernel,
        grid=(tokens // BLOCK,),
        in_specs=[
            pl.BlockSpec((BLOCK, width), lambda i: (i, 0)),
            pl.BlockSpec((1, width), lambda i: (0, 0)),
            pl.BlockSpec((width, QKV), lambda i: (0, 0)),
            pl.BlockSpec((1, QKV), lambda i: (0, 0)),
            pl.BlockSpec((BLOCK, LANES), lambda i: (i % steps, 0)),
            pl.BlockSpec((BLOCK, LANES), lambda i: (i % steps, 0)),
        ],
        out_specs=[
            pl.BlockSpec((BLOCK, width), lambda i: (i, 0)),
            pl.BlockSpec((BLOCK, QKV), lambda i: (i, 0)),
        ],
        out_shape=[
            jax.ShapeDtypeStruct((tokens, width), jnp.bfloat16),
            jax.ShapeDtypeStruct((tokens, QKV), jnp.bfloat16),
        ],
        compiler_params=pltpu.CompilerParams(vmem_limit_bytes=VMEM_BYTES),
        cost_estimate=cost(2 * tokens * width * QKV * 2, 8 * tokens * QKV),
        name="joint_projection",
    )(inputs, gain, weight, bias, cosine, sine)


def select_head(values, head):
    return jnp.where(head // GROUP == 0, values[:, :HD], values[:, HD:])


def attend_kernel(first, q_ref, k_ref, v_ref, out_ref):
    pair = pl.program_id(1) + first
    scale = HD ** (-0.5)
    for e in range(2):
        keys = select_head(k_ref[...], 2 * pair + e)
        values = select_head(v_ref[...], 2 * pair + e)
        for i in range(SEQ_LEN // BLOCK):
            rows, end = pl.ds(i * BLOCK, BLOCK), (i + 1) * BLOCK
            query = q_ref[rows, e * HD : (e + 1) * HD] * jnp.bfloat16(scale)
            scores = dot(query, keys[:end], NT)
            rows_at = i * BLOCK + lax.broadcasted_iota(jnp.int32, scores.shape, 0)
            keys_at = lax.broadcasted_iota(jnp.int32, scores.shape, 1)
            scores = jnp.where(keys_at <= rows_at, scores, MASKED)
            weights = jnp.exp(scores - jnp.max(scores, -1, keepdims=True))
            total = jnp.sum(weights, -1, keepdims=True)
            attended = dot(low(weights), values[:end]) / total
            out_ref[rows, e * HD : (e + 1) * HD] = low(attended)


def attend(joint, first, pairs):
    tokens = joint.shape[0]
    seqs = tokens // SEQ_LEN
    return pl.pallas_call(
        functools.partial(attend_kernel, first),
        grid=(seqs, pairs),
        in_specs=[
            pl.BlockSpec((SEQ_LEN, LANES), lambda s, p: (s, p + first)),
            pl.BlockSpec((SEQ_LEN, LANES), lambda s, p: (s, WIDTH // LANES)),
            pl.BlockSpec((SEQ_LEN, LANES), lambda s, p: (s, QK_WIDTH // LANES)),
        ],
        out_specs=pl.BlockSpec((SEQ_LEN, LANES), lambda s, p: (s, p)),
        out_shape=jax.ShapeDtypeStruct((tokens, pairs * LANES), jnp.bfloat16),
        compiler_params=pltpu.CompilerParams(vmem_limit_bytes=VMEM_BYTES),
        cost_estimate=cost(
            tokens * SEQ_LEN * pairs * 1024, 8 * tokens * pairs * LANES, tokens * 1024 * pairs
        ),
        name="attend",
    )(joint, joint, joint)


def attend_back_kernel(first, last, *refs):
    if first > 0:
        q_ref, k_ref, v_ref, g_ref, cos_ref, sin_ref, key_in, value_in = refs[:8]
    else:
        q_ref, k_ref, v_ref, g_ref, cos_ref, sin_ref = refs[:6]
    dq_ref, dk_ref, dv_ref, key_sum, value_sum = refs[-5:]
    pair = pl.program_id(1) + first
    scale = HD ** (-0.5)

    @pl.when(pair == first)
    def _():
        key_sum[...] = key_in[...] if first > 0 else jnp.zeros_like(key_sum)
        value_sum[...] = value_in[...] if first > 0 else jnp.zeros_like(value_sum)

    for i in range(SEQ_LEN // BLOCK):
        rows, end = pl.ds(i * BLOCK, BLOCK), (i + 1) * BLOCK
        parts = []
        for e in range(2):
            head = 2 * pair + e
            kv = head // GROUP
            keys = select_head(k_ref[:end, :], head)
            values = select_head(v_ref[:end, :], head)
            query = q_ref[rows, e * HD : (e + 1) * HD] * jnp.bfloat16(scale)
            grad = g_ref[rows, e * HD : (e + 1) * HD]
            scores = dot(keys, query, NT)
            keys_at = lax.broadcasted_iota(jnp.int32, scores.shape, 0)
            rows_at = i * BLOCK + lax.broadcasted_iota(jnp.int32, scores.shape, 1)
            scores = jnp.where(keys_at <= rows_at, scores, MASKED)
            weights = jnp.exp(scores - jnp.max(scores, 0, keepdims=True))
            prob = weights * (1.0 / jnp.sum(weights, 0, keepdims=True))
            prob_grad = dot(values, grad, NT)
            inner = jnp.sum(prob * prob_grad, 0, keepdims=True)
            score_grad = low(prob * (prob_grad - inner))
            value_sum[kv, :end, :] += dot(low(prob), grad)
            key_sum[kv, :end, :] += dot(score_grad, query)
            parts.append(dot(keys, score_grad, TN))
        query_grad = jnp.transpose(jnp.concatenate(parts, 0)) * scale
        turned = turn_pairs(query_grad, cos_ref[rows, :], -sin_ref[rows, :])
        dq_ref[rows, :] = low(turned)

    @pl.when(pair == last)
    def _():
        if last < QH // 2 - 1:
            dk_ref[...] = key_sum[...]
            dv_ref[...] = value_sum[...]
            return
        key_grad = jnp.concatenate([key_sum[0], key_sum[1]], 1)
        dk_ref[...] = low(turn_pairs(key_grad, cos_ref[...], -sin_ref[...]))
        dv_ref[...] = low(jnp.concatenate([value_sum[0], value_sum[1]], 1))


def attend_back(joint, grad, cosine, sine, first, pairs, sums):
    tokens = joint.shape[0]
    last = first + pairs - 1
    ends = last == QH // 2 - 1
    seqs = tokens // SEQ_LEN
    block = (SEQ_LEN, LANES)
    held = pl.BlockSpec((KVH, SEQ_LEN, HD), lambda s, p: (s, 0, 0))
    return pl.pallas_call(
        functools.partial(attend_back_kernel, first, last),
        grid=(seqs, pairs),
        in_specs=[
            pl.BlockSpec(block, lambda s, p: (s, p + first)),
            pl.BlockSpec(block, lambda s, p: (s, WIDTH // LANES)),
            pl.BlockSpec(block, lambda s, p: (s, QK_WIDTH // LANES)),
            pl.BlockSpec(block, lambda s, p: (s, p + first)),
            pl.BlockSpec(block, lambda s, p: (0, 0)),
            pl.BlockSpec(block, lambda s, p: (0, 0)),
        ]
        + ([] if sums is None else [held, held]),
        out_specs=[
            pl.BlockSpec(block, lambda s, p: (s, p)),
        ]
        + [pl.BlockSpec(block, lambda s, p: (s, 0)) if ends else held] * 2,
        out_shape=[
            jax.ShapeDtypeStruct((tokens, pairs * LANES), jnp.bfloat16),
        ]
        + [
            jax.ShapeDtypeStruct((tokens, KV_WIDTH), jnp.bfloat16)
            if ends
            else jax.ShapeDtypeStruct((seqs * KVH, SEQ_LEN, HD), jnp.float32)
        ]
        * 2,
        scratch_shapes=[
            pltpu.VMEM((KVH, SEQ_LEN, HD), jnp.float32),
            pltpu.VMEM((KVH, SEQ_LEN, HD), jnp.float32),
        ],
        compiler_params=pltpu.CompilerParams(vmem_limit_bytes=VMEM_BYTES),
        cost_estimate=cost(
            tokens * SEQ_LEN * pairs * 2560, 8 * tokens * pairs * LANES, tokens * 1024 * pairs
        ),
        name="attend_back",
    )(joint, joint, joint, grad, cosine, sine, *(sums or ()))


def feed_kernel(
    act_ref, cot_ref, weight_ref, mix_ref, grad_ref, hid_ref, dgate_ref, dup_ref
):
    act, cot = act_ref[...], cot_ref[...]
    gate_ref, up_ref, down_ref = weight_ref.at[0], weight_ref.at[1], weight_ref.at[2]
    gate = dot(act, gate_ref[...])
    up_part = dot(act, up_ref[...])
    hidden_grad = dot(cot, down_ref[...])
    sigma = jax.nn.sigmoid(gate)
    silu = gate * sigma
    hidden = low(silu * up_part)
    gate_grad = low(hidden_grad * up_part * sigma * (1.0 + gate * (1.0 - sigma)))
    up_grad = low(hidden_grad * silu)
    hid_ref[...] = hidden
    dgate_ref[...] = gate_grad
    dup_ref[...] = up_grad
    mix_ref[...] = low(dot(hidden, down_ref[...], NT))
    grad_ref[...] = low(dot(gate_grad, gate_ref[...], NT) + dot(up_grad, up_ref[...], NT))


def feed(act, cot, weights):
    tokens, width = act.shape
    inner = weights.shape[2]
    narrow = pl.BlockSpec((BLOCK, width), lambda i: (i, 0))
    wide = pl.BlockSpec((BLOCK, inner), lambda i: (i, 0))
    weight = pl.BlockSpec((3, width, inner), lambda i: (0, 0, 0))
    return pl.pallas_call(
        feed_kernel,
        grid=(tokens // BLOCK,),
        in_specs=[narrow, narrow, weight],
        out_specs=[narrow, narrow, wide, wide, wide],
        out_shape=[jax.ShapeDtypeStruct((tokens, width), jnp.bfloat16)] * 2
        + [jax.ShapeDtypeStruct((tokens, inner), jnp.bfloat16)] * 3,
        compiler_params=pltpu.CompilerParams(vmem_limit_bytes=VMEM_BYTES),
        cost_estimate=cost(
            12 * tokens * width * inner, 2 * tokens * (4 * width + 3 * inner), tokens * inner
        ),
        name="feed",
    )(act, cot, weights)


def normalize_back(values, inverse, gain, upstream):
    weighted = upstream * gain
    inner = jnp.mean(weighted * values, -1, keepdims=True)
    value_grad = inverse * weighted - values * inverse * inverse * inverse * inner
    gain_grad = jnp.sum(upstream * values * inverse, 0)
    return (value_grad, gain_grad)


def inverse_of(values):
    return lax.rsqrt(jnp.mean(values * values, -1, keepdims=True) + EPS)


def rotary_tables():
    freq = BASE ** (-(jnp.arange(HD // 2, dtype=jnp.float32) * 2.0 / HD))
    angle = jnp.arange(SEQ_LEN, dtype=jnp.float32)[:, None] * freq[None, :]
    cosine, sine = jnp.cos(angle), jnp.sin(angle)
    cosine = jnp.concatenate([cosine] * 4, 1)
    sine = jnp.concatenate([-sine, sine, -sine, sine], 1)
    return cosine, sine


def body(
    sizes,
    block_input,
    first_gain,
    joint_weight,
    joint_bias,
    output_weight,
    second_gain,
    gate_weight,
    up_weight,
    down_weight,
    cotangent,
):
    grid = Grid(sizes)
    shard = gate_weight.shape[1]
    inner = -(-shard // LANES) * LANES
    wide = ((0, 0), (0, inner - shard))
    gain_size, bias_size = first_gain.shape[0], joint_bias.shape[0]
    stretch = (0, bias_size - gain_size)
    small = jnp.stack([joint_bias, jnp.pad(first_gain, stretch), jnp.pad(second_gain, stretch)])
    small = grid.gather_small(small)
    bias_full = small[:, 0].reshape(1, -1).astype(jnp.float32)
    first_scale = small[:, 1, :gain_size].reshape(1, -1).astype(jnp.float32)
    second_scale = small[:, 2, :gain_size].reshape(1, -1).astype(jnp.float32)
    columns = jnp.concatenate([joint_weight, output_weight], 1)
    blocks, last = grid.gather_all(columns)
    joint_full = jnp.concatenate([block[:, :bias_size] for block in blocks], 1)
    output_full = jnp.concatenate([block[:, bias_size:] for block in blocks], 1)
    cosine, sine = rotary_tables()
    size = sizes["col"]
    cot_near = flip(cotangent, "col", size, 1)
    cot_far = flip(cotangent, "col", size, 2)

    first_act, joint = joint_projection(
        block_input, first_scale, joint_full, bias_full, cosine, sine
    )
    attended_low = attend(joint, 0, 4)
    attended_high = attend(joint, 4, 3)
    attended = jnp.concatenate([attended_low, attended_high], 1)
    inputs = block_input.astype(jnp.float32)
    resid = inputs + dot(attended, output_full)
    second_inverse = inverse_of(resid)
    second_act = low(resid * second_inverse * second_scale)
    weights = jnp.stack([gate_weight, up_weight, down_weight.T])
    weights = after(jnp.pad(weights, ((0, 0),) + wide), last)
    holds = (joint, attended_low, attended_high, second_act)
    weights, _ = grid.gather_rows(weights, 1, holds)

    act_near = flip(second_act, "col", size, 1)
    act_far = flip(second_act, "col", size, 2)
    cot_last = flip(after(cot_far, joint), "col", size, 1)
    fed_own = feed(second_act, cotangent, weights)
    fed_near = feed(act_near, cot_near, weights)
    act_far = after(act_far, fed_near[0])
    act_last = flip(act_far, "col", size, 1)
    fed_far = feed(act_far, cot_far, weights)
    fed_last = feed(act_last, cot_last, weights)
    fed = (fed_own, fed_near, fed_far, fed_last)

    got_near = flip(fed_near[1], "col", size, 1)
    got_last = flip(fed_last[1], "col", size, 1)
    got_far = flip(add(fed_far[1], got_last), "col", size, 2)

    act_all = jnp.concatenate([second_act, act_near, act_far, act_last], 0)
    cot_all = jnp.concatenate([cotangent, cot_near, cot_far, cot_last], 0)
    hidden, gate_grad, up_grad = (
        jnp.concatenate([item[at] for item in fed], 0) for at in (2, 3, 4)
    )
    down_part = low(dot(cot_all, hidden, TN))
    down_mine, down_got = grid.swap_halves(down_part)
    gate_part = low(dot(act_all, after(gate_grad, down_part), TN))
    gate_mine, gate_got = grid.swap_halves(gate_part)
    up_part = low(dot(act_all, after(up_grad, gate_part), TN))
    up_mine, up_got = grid.swap_halves(up_part)

    got_far = after(got_far, up_part)
    second_grad = fed_own[1].astype(jnp.float32) + got_near.astype(jnp.float32)
    second_grad = second_grad + got_far.astype(jnp.float32)
    resid_norm_grad, second_gain_grad = normalize_back(
        resid, second_inverse, second_scale, second_grad
    )
    resid_grad = cotangent.astype(jnp.float32) + resid_norm_grad
    proj_grad = low(resid_grad)
    attended_grad = low(dot(proj_grad, output_full, NT))

    mix_last = flip(after(fed_last[0], got_far), "col", size, 1)
    mix_near = flip(after(fed_near[0], got_far), "col", size, 1)

    back = attend_back(joint, attended_grad, cosine, sine, 0, 3, None)
    query_low, sums = back[0], back[1:]
    mix_far = flip(add(fed_far[0], after(mix_last, attended_grad)), "col", size, 2)
    down_mine = add(down_mine, after(down_got, up_part))
    down_total = grid.scatter_half(down_mine, (attended_grad, query_low, query_low))
    query_mid, *sums = attend_back(joint, attended_grad, cosine, sine, 3, 2, sums)
    gate_mine = add(gate_mine, after(gate_got, query_low))
    up_mine = add(up_mine, after(up_got, query_mid))
    query_high, key_grad, value_grad = attend_back(
        joint, attended_grad, cosine, sine, 5, 2, sums
    )
    both = jnp.concatenate([gate_mine, up_mine], 1)
    both_total = grid.scatter_half(both, (query_high, query_high, query_high))
    down_w_grad = grid.both_halves(after(down_total, query_mid))

    joint_grad = jnp.concatenate([query_low, query_mid, query_high, key_grad, value_grad], 1)
    joint_part = low(dot(first_act, joint_grad, TN))
    output_part = low(dot(attended, proj_grad, TN))
    pieces = [
        jnp.concatenate(
            [
                joint_part[:, j * bias_size : (j + 1) * bias_size],
                output_part[:, j * gain_size : (j + 1) * gain_size],
            ],
            1,
        )
        for j in range(size)
    ]
    block_grad = grid.scatter_all(pieces)
    joint_w_grad, output_w_grad = block_grad[:, :bias_size], block_grad[:, bias_size:]
    bias_grad = jnp.sum(joint_grad.astype(jnp.float32), 0)
    first_grad = dot(joint_grad, joint_full, NT)
    first_inverse = inverse_of(inputs)
    input_norm_grad, first_gain_grad = normalize_back(
        inputs, first_inverse, first_scale, first_grad
    )
    input_grad = low(resid_grad + input_norm_grad)
    totals = grid.sum_small(jnp.concatenate([bias_grad, first_gain_grad, second_gain_grad]))

    mix_far = after(mix_far, query_high).astype(jnp.float32)
    mixed = fed_own[0].astype(jnp.float32) + mix_near.astype(jnp.float32) + mix_far
    block_output = low(resid + mixed)
    half = both_total.shape[0] // 2
    other = flip(both_total, "dp", sizes["dp"], 1)
    gate_w_grad, up_w_grad = (
        join(both_total[at : at + half], other[at : at + half], grid.odd_dp == 1, 0)
        for at in (0, half)
    )

    def own(start, size):
        part = size // grid.col
        return lax.dynamic_slice_in_dim(totals, start + grid.at_col * part, part, 0)

    model = first_gain_grad.shape[0]
    wide_out = lambda values: values.astype(jnp.float32)
    return (
        block_output,
        input_grad,
        own(QKV, model),
        wide_out(joint_w_grad),
        own(0, QK_WIDTH),
        own(QK_WIDTH, KV_WIDTH),
        wide_out(output_w_grad),
        own(QKV + model, model),
        wide_out(gate_w_grad[:, :shard]),
        wide_out(up_w_grad[:, :shard]),
        wide_out(down_w_grad[:, :shard].T),
    )


def solution(mesh):
    tokens = P(("dp", "row", "col"), None)
    return jax.shard_map(
        functools.partial(body, dict(mesh.shape)),
        mesh=mesh,
        in_specs=(
            tokens,
            P("col"),
            P("row", "col"),
            P("col"),
            P("row", "col"),
            P("col"),
            P("row", "col"),
            P("row", "col"),
            P("col", "row"),
            tokens,
        ),
        out_specs=(
            tokens,
            tokens,
            P("col"),
            P("row", "col"),
            P("col"),
            P("col"),
            P("row", "col"),
            P("col"),
            P("row", "col"),
            P("row", "col"),
            P("col", "row"),
        ),
        check_vma=False,
    )
```

```python
import functools

import jax
import jax.numpy as jnp
from jax import lax
from jax.experimental import pallas as pl
from jax.experimental.pallas import tpu as pltpu
from jax.sharding import PartitionSpec as P

QH = 14
KVH = 2
HD = 64
SEQ_LEN = 1024
GROUP = QH // KVH
WIDTH = QH * HD
KV_WIDTH = KVH * HD
QK_WIDTH = WIDTH + KV_WIDTH
QKV = QK_WIDTH + KV_WIDTH

EPS = 1e-06
BASE = 1000000.0
MASKED = -1e30
LANES = 128
BLOCK = 256

NN = (((1,), (0,)), ((), ()))
NT = (((1,), (1,)), ((), ()))
TN = (((0,), (0,)), ((), ()))
VMEM_BYTES = 56 * 1024 * 1024


def dot(left, right, dims=NN):
    return lax.dot_general(left, right, dims, preferred_element_type=jnp.float32)


def low(values):
    return values.astype(jnp.bfloat16)


def add(left, right):
    return low(left.astype(jnp.float32) + right.astype(jnp.float32))


def cost(flops, moved, transcendentals=0):
    return pl.CostEstimate(
        flops=int(flops) // 1000,
        bytes_accessed=int(moved) // 1000,
        transcendentals=int(transcendentals) // 1000,
    )


def flip(values, axis, size, bit):
    return lax.ppermute(values, axis, [(i, i ^ bit) for i in range(size)])


def shift(values, axis, size):
    return lax.ppermute(values, axis, [(i, (i + 1) % size) for i in range(size)])


def join(mine, other, odd, axis):
    first = jnp.where(odd, other, mine)
    second = jnp.where(odd, mine, other)
    return jnp.concatenate([first, second], axis)


def half_of(values, which, axis):
    size = values.shape[axis] // 2
    return lax.dynamic_slice_in_dim(values, which * size, size, axis)


def after(values, done):
    return lax.optimization_barrier((values, done))[0] if jax.tree.leaves(done) else values


class Grid:
    def __init__(self, sizes):
        self.dp, self.row, self.col = sizes["dp"], sizes["row"], sizes["col"]
        self.at_dp = lax.axis_index("dp")
        self.at_row = lax.axis_index("row")
        self.at_col = lax.axis_index("col")
        self.odd_dp = self.at_dp % 2
        self.core = self.at_col % 2
        self.pair = self.at_col // 2

    def gather_half_rows(self, block, axis):
        mine = half_of(block, self.odd_dp, axis)
        pairs = []
        for _ in range(1, self.row):
            mine = shift(mine, "row", self.row)
            pairs.append((mine, flip(mine, "dp", self.dp, 1)))
        return pairs, mine

    def gather_columns(self, block, holds):
        other = flip(block, "col", self.col, 2)
        both = join(block[None], other[None], self.pair == 1, 0)
        size = both.shape[1]
        full = jnp.zeros((2, size * self.row, both.shape[2]), both.dtype)
        full = lax.dynamic_update_slice_in_dim(full, both, self.at_row * size, 1)
        mine = half_of(both, self.odd_dp, 1)
        for step in range(1, self.row):
            mine = shift(mine, "row", self.row)
            mine = after(mine, holds.get(step, ()))
            whole = join(mine, flip(mine, "dp", self.dp, 1), self.odd_dp == 1, 1)
            at = (self.at_row - step) % self.row
            full = lax.dynamic_update_slice_in_dim(full, whole, at * size, 1)
        return full, mine

    def gather_small(self, block):
        size = block.shape[1]
        both = join(block, flip(block, "col", self.col, 2), self.pair == 1, 1)
        other = flip(both, "col", self.col, 1)
        first = jnp.where(self.core == 1, other, both)
        second = jnp.where(self.core == 1, both, other)
        pieces = [first[:, :size], second[:, :size], first[:, size:], second[:, size:]]
        return jnp.concatenate(pieces, 1)

    def swap_halves(self, part):
        size = part.shape[0] // self.row
        blocks = part.reshape(self.row, size, part.shape[1])
        mine = half_of(blocks, self.odd_dp, 1)
        theirs = half_of(blocks, 1 - self.odd_dp, 1)
        return mine, flip(theirs, "dp", self.dp, 1), theirs

    def sum_pairs(self, total):
        bit = 2
        while bit < self.dp:
            total = add(total, flip(total, "dp", self.dp, bit))
            bit *= 2
        return total

    def own_block(self, mine, step):
        at = (self.at_row - step) % self.row
        return lax.dynamic_index_in_dim(mine, at, 0, False)

    def ring_start(self, mine):
        sent = self.own_block(mine, 1)
        return shift(sent, "row", self.row), sent

    def ring_step(self, mine, got, step):
        total = add(got, self.own_block(mine, step + 1))
        if step < self.row - 1:
            return total, shift(total, "row", self.row)
        return self.sum_pairs(total)

    def scatter_direct(self, mine):
        total = lax.dynamic_index_in_dim(mine, self.at_row, 0, False).astype(jnp.float32)
        for step in range(1, self.row):
            to = (self.at_row + step) % self.row
            block = lax.dynamic_index_in_dim(mine, to, 0, False)
            pairs = [(i, (i + step) % self.row) for i in range(self.row)]
            total = total + lax.ppermute(block, "row", pairs).astype(jnp.float32)
        return self.sum_pairs(low(total))

    def sum_axis(self, values, axis):
        size = getattr(self, axis)
        return [
            lax.ppermute(values, axis, [(i, (i + step) % size) for i in range(size)])
            for step in range(1, size)
        ]

    def both_halves(self, total):
        other = flip(total, "dp", self.dp, 1)
        return join(total, other, self.odd_dp == 1, 0)

    def core_parts(self, part):
        size = part.shape[0] // self.col
        pieces = part.reshape(self.col, size, part.shape[1])
        evens, odds = jnp.stack([pieces[0], pieces[2]]), jnp.stack([pieces[1], pieces[3]])
        mine = jnp.where(self.core == 1, odds, evens)
        theirs = jnp.where(self.core == 1, evens, odds)
        return mine, flip(theirs, "col", self.col, 1), theirs

    def pair_parts(self, both):
        mine = jnp.where(self.pair == 1, both[1], both[0])
        theirs = jnp.where(self.pair == 1, both[0], both[1])
        return mine, flip(theirs, "col", self.col, 2), theirs


def turn_pairs(values, cosine, sine):
    lane = lax.broadcasted_iota(jnp.int32, values.shape, 1)
    before = pltpu.roll(values, HD // 2, 1)
    after = pltpu.roll(values, LANES - HD // 2, 1)
    partner = jnp.where(lane % HD < HD // 2, after, before)
    return values * cosine + partner * sine


def place_kernel(joint_size, mine_ref, other_ref, joint_ref, output_ref):
    core = lax.axis_index("col") % 2
    size = mine_ref.shape[2]
    rest = size - joint_size

    def place(first_ref, second_ref):
        pieces = (first_ref[0], second_ref[0], first_ref[1], second_ref[1])
        for j, piece in enumerate(pieces):
            joint_ref[:, j * joint_size : (j + 1) * joint_size] = piece[:, :joint_size]
            output_ref[:, j * rest : (j + 1) * rest] = piece[:, joint_size:]

    @pl.when(core == 0)
    def _():
        place(mine_ref, other_ref)

    @pl.when(core == 1)
    def _():
        place(other_ref, mine_ref)


def place_columns(mine, other, joint_size):
    _, rows, size = mine.shape
    step = rows // 4
    block = pl.BlockSpec((2, step, size), lambda i: (0, i, 0))
    widths = (4 * joint_size, 4 * (size - joint_size))
    return pl.pallas_call(
        functools.partial(place_kernel, joint_size),
        grid=(4,),
        in_specs=[block, block],
        out_specs=[pl.BlockSpec((step, width), lambda i: (i, 0)) for width in widths],
        out_shape=[jax.ShapeDtypeStruct((rows, width), jnp.bfloat16) for width in widths],
        compiler_params=pltpu.CompilerParams(vmem_limit_bytes=VMEM_BYTES),
        cost_estimate=cost(0, 16 * rows * size),
        name="place_columns",
    )(mine, other)


def joint_kernel(x_ref, gain_ref, weight_ref, bias_ref, cos_ref, sin_ref, act_ref, out_ref):
    inputs = x_ref[...].astype(jnp.float32)
    inverse = lax.rsqrt(jnp.mean(inputs * inputs, -1, keepdims=True) + EPS)
    act = low(inputs * inverse * gain_ref[...])
    act_ref[...] = act
    joint = dot(act, weight_ref[...]) + bias_ref[...]
    cosine, sine = cos_ref[...], sin_ref[...]
    for start in range(0, QK_WIDTH, LANES):
        turned = turn_pairs(joint[:, start : start + LANES], cosine, sine)
        out_ref[:, start : start + LANES] = low(turned)
    out_ref[:, QK_WIDTH:] = low(joint[:, QK_WIDTH:])


def joint_projection(inputs, gain, weight, bias, cosine, sine):
    tokens, width = inputs.shape
    steps = SEQ_LEN // BLOCK
    return pl.pallas_call(
        joint_kernel,
        grid=(tokens // BLOCK,),
        in_specs=[
            pl.BlockSpec((BLOCK, width), lambda i: (i, 0)),
            pl.BlockSpec((1, width), lambda i: (0, 0)),
            pl.BlockSpec((width, QKV), lambda i: (0, 0)),
            pl.BlockSpec((1, QKV), lambda i: (0, 0)),
            pl.BlockSpec((BLOCK, LANES), lambda i: (i % steps, 0)),
            pl.BlockSpec((BLOCK, LANES), lambda i: (i % steps, 0)),
        ],
        out_specs=[
            pl.BlockSpec((BLOCK, width), lambda i: (i, 0)),
            pl.BlockSpec((BLOCK, QKV), lambda i: (i, 0)),
        ],
        out_shape=[
            jax.ShapeDtypeStruct((tokens, width), jnp.bfloat16),
            jax.ShapeDtypeStruct((tokens, QKV), jnp.bfloat16),
        ],
        compiler_params=pltpu.CompilerParams(vmem_limit_bytes=VMEM_BYTES),
        cost_estimate=cost(2 * tokens * width * QKV * 2, 8 * tokens * QKV),
        name="joint_projection",
    )(inputs, gain, weight, bias, cosine, sine)


def select_head(values, head):
    return jnp.where(head // GROUP == 0, values[:, :HD], values[:, HD:])


def attend_kernel(first, q_ref, k_ref, v_ref, out_ref):
    pair = pl.program_id(1) + first
    scale = HD ** (-0.5)
    for e in range(2):
        keys = select_head(k_ref[...], 2 * pair + e)
        values = select_head(v_ref[...], 2 * pair + e)
        for i in range(SEQ_LEN // BLOCK):
            rows, end = pl.ds(i * BLOCK, BLOCK), (i + 1) * BLOCK
            query = q_ref[rows, e * HD : (e + 1) * HD] * jnp.bfloat16(scale)
            scores = dot(query, keys[:end], NT)
            rows_at = i * BLOCK + lax.broadcasted_iota(jnp.int32, scores.shape, 0)
            keys_at = lax.broadcasted_iota(jnp.int32, scores.shape, 1)
            scores = jnp.where(keys_at <= rows_at, scores, MASKED)
            weights = jnp.exp(scores - jnp.max(scores, -1, keepdims=True))
            total = jnp.sum(weights, -1, keepdims=True)
            attended = dot(low(weights), values[:end]) / total
            out_ref[rows, e * HD : (e + 1) * HD] = low(attended)


def attend(joint, first, pairs):
    tokens = joint.shape[0]
    seqs = tokens // SEQ_LEN
    return pl.pallas_call(
        functools.partial(attend_kernel, first),
        grid=(seqs, pairs),
        in_specs=[
            pl.BlockSpec((SEQ_LEN, LANES), lambda s, p: (s, p + first)),
            pl.BlockSpec((SEQ_LEN, LANES), lambda s, p: (s, WIDTH // LANES)),
            pl.BlockSpec((SEQ_LEN, LANES), lambda s, p: (s, QK_WIDTH // LANES)),
        ],
        out_specs=pl.BlockSpec((SEQ_LEN, LANES), lambda s, p: (s, p)),
        out_shape=jax.ShapeDtypeStruct((tokens, pairs * LANES), jnp.bfloat16),
        compiler_params=pltpu.CompilerParams(vmem_limit_bytes=VMEM_BYTES),
        cost_estimate=cost(
            tokens * SEQ_LEN * pairs * 1024, 8 * tokens * pairs * LANES, tokens * 1024 * pairs
        ),
        name="attend",
    )(joint, joint, joint)


def attend_back_kernel(first, last, *refs):
    q_ref, k_ref, v_ref, g_ref, cos_ref, sin_ref = refs[:6]
    if first > 0:
        key_in, value_in = refs[7:9]
    ends = last == QH // 2 - 1
    if not ends:
        dk_ref, dv_ref = refs[-4:-2]
    dq_ref = refs[-3] if ends else refs[-5]
    key_sum, value_sum = refs[-2:]
    pair = pl.program_id(1) + first
    scale = HD ** (-0.5)

    @pl.when(pair == first)
    def _():
        key_sum[...] = key_in[...] if first > 0 else jnp.zeros_like(key_sum)
        value_sum[...] = value_in[...] if first > 0 else jnp.zeros_like(value_sum)

    @pl.when(pair <= last)
    def _():
        for i in range(SEQ_LEN // BLOCK):
            rows, end = pl.ds(i * BLOCK, BLOCK), (i + 1) * BLOCK
            parts = []
            for e in range(2):
                head = 2 * pair + e
                kv = head // GROUP
                keys = select_head(k_ref[:end, :], head)
                values = select_head(v_ref[:end, :], head)
                query = q_ref[rows, e * HD : (e + 1) * HD] * jnp.bfloat16(scale)
                grad = g_ref[rows, e * HD : (e + 1) * HD]
                scores = dot(keys, query, NT)
                keys_at = lax.broadcasted_iota(jnp.int32, scores.shape, 0)
                rows_at = i * BLOCK + lax.broadcasted_iota(jnp.int32, scores.shape, 1)
                scores = jnp.where(keys_at <= rows_at, scores, MASKED)
                weights = jnp.exp(scores - jnp.max(scores, 0, keepdims=True))
                prob = weights * (1.0 / jnp.sum(weights, 0, keepdims=True))
                prob_grad = dot(values, grad, NT)
                inner = jnp.sum(prob * prob_grad, 0, keepdims=True)
                score_grad = low(prob * (prob_grad - inner))
                value_sum[kv, :end, :] += dot(low(prob), grad)
                key_sum[kv, :end, :] += dot(score_grad, query)
                parts.append(dot(keys, score_grad, TN))
            query_grad = jnp.transpose(jnp.concatenate(parts, 0)) * scale
            turned = turn_pairs(query_grad, cos_ref[rows, :], -sin_ref[rows, :])
            dq_ref[rows, :] = low(turned)

    if not ends:

        @pl.when(pair == last)
        def _():
            dk_ref[...] = key_sum[...]
            dv_ref[...] = value_sum[...]

        return

    @pl.when(pair == last + 1)
    def _():
        key_grad = jnp.concatenate([key_sum[0], key_sum[1]], 1)
        dq_ref[...] = low(turn_pairs(key_grad, cos_ref[...], -sin_ref[...]))

    @pl.when(pair == last + 2)
    def _():
        dq_ref[...] = low(jnp.concatenate([value_sum[0], value_sum[1]], 1))


def attend_back(joint, grad, cosine, sine, first, pairs, sums):
    tokens = joint.shape[0]
    last = first + pairs - 1
    ends = last == QH // 2 - 1
    seqs = tokens // SEQ_LEN
    steps = pairs + 2 if ends else pairs
    block = (SEQ_LEN, LANES)
    held = pl.BlockSpec((KVH, SEQ_LEN, HD), lambda s, p: (s, 0, 0))
    return pl.pallas_call(
        functools.partial(attend_back_kernel, first, last),
        grid=(seqs, steps),
        in_specs=[
            pl.BlockSpec(block, lambda s, p: (s, jnp.minimum(p + first, last))),
            pl.BlockSpec(block, lambda s, p: (s, WIDTH // LANES)),
            pl.BlockSpec(block, lambda s, p: (s, QK_WIDTH // LANES)),
            pl.BlockSpec(block, lambda s, p: (s, jnp.minimum(p + first, last))),
            pl.BlockSpec(block, lambda s, p: (0, 0)),
            pl.BlockSpec(block, lambda s, p: (0, 0)),
        ]
        + ([pl.BlockSpec(memory_space=pl.ANY), held, held] if sums else []),
        out_specs=[pl.BlockSpec(block, lambda s, p: (s, p + first))]
        + ([] if ends else [held] * 2),
        out_shape=[jax.ShapeDtypeStruct((tokens, QKV), jnp.bfloat16)]
        + [jax.ShapeDtypeStruct((seqs * KVH, SEQ_LEN, HD), jnp.float32)] * (0 if ends else 2),
        input_output_aliases={6: 0} if sums else {},
        scratch_shapes=[
            pltpu.VMEM((KVH, SEQ_LEN, HD), jnp.float32),
            pltpu.VMEM((KVH, SEQ_LEN, HD), jnp.float32),
        ],
        compiler_params=pltpu.CompilerParams(vmem_limit_bytes=VMEM_BYTES),
        cost_estimate=cost(
            tokens * SEQ_LEN * pairs * 2560, 8 * tokens * pairs * LANES, tokens * 1024 * pairs
        ),
        name="attend_back",
    )(joint, joint, joint, grad, cosine, sine, *sums)


def feed_kernel(sizes, held, *refs):
    rows, dps = sizes
    pieces = 2 * rows - 1
    act_ref, cot_ref = refs[:2]
    parts = refs[2 : 2 + pieces]
    outs = refs[2 + pieces + held :]
    mix_ref, grad_ref, hid_ref, dgate_ref, dup_ref, act_out, cot_out, weight_ref, sems = outs
    size = parts[0].shape[1]
    half = size // 2

    @pl.when(pl.program_id(0) == 0)
    def _():
        row, odd = lax.axis_index("row"), lax.axis_index("dp") % 2
        copies = []
        for at, part in enumerate(parts):
            step = (at + 1) // 2
            start = (row + rows - step) % rows * size
            if at > 0:
                start = start + half * (odd if at % 2 == 1 else 1 - odd)
            span = pl.ds(pl.multiple_of(start, 16), part.shape[1])
            copies.append(pltpu.make_async_copy(part, weight_ref.at[:, span, :], sems.at[at]))
        for copy in copies:
            copy.start()
        for copy in copies:
            copy.wait()

    act, cot = act_ref[...], cot_ref[...]
    act_out[...] = act
    cot_out[...] = cot
    gate_ref, up_ref, down_ref = weight_ref.at[0], weight_ref.at[1], weight_ref.at[2]
    gate = dot(act, gate_ref[...])
    up_part = dot(act, up_ref[...])
    hidden_grad = dot(cot, down_ref[...])
    sigma = jax.nn.sigmoid(gate)
    silu = gate * sigma
    hidden = low(silu * up_part)
    gate_grad = low(hidden_grad * up_part * sigma * (1.0 + gate * (1.0 - sigma)))
    up_grad = low(hidden_grad * silu)
    hid_ref[...] = hidden
    dgate_ref[...] = gate_grad
    dup_ref[...] = up_grad
    mix_ref[...] = low(dot(hidden, down_ref[...], NT))
    grad_ref[...] = low(dot(gate_grad, gate_ref[...], NT) + dot(up_grad, up_ref[...], NT))


def feed(sizes, slot, slots, act, cot, parts, held):
    tokens, width = act.shape
    inner = parts[0].shape[2]
    steps = tokens // BLOCK
    narrow = pl.BlockSpec((BLOCK, width), lambda i: (i, 0))
    narrow_at = pl.BlockSpec((BLOCK, width), lambda i: (i + slot * steps, 0))
    wide_at = pl.BlockSpec((BLOCK, inner), lambda i: (i + slot * steps, 0))
    anywhere = pl.BlockSpec(memory_space=pl.ANY)
    first = 2 + len(parts)
    return pl.pallas_call(
        functools.partial(feed_kernel, sizes, len(held)),
        grid=(steps,),
        in_specs=[narrow, narrow] + [anywhere] * (len(parts) + len(held)),
        out_specs=[narrow, narrow, wide_at, wide_at, wide_at, narrow_at, narrow_at],
        out_shape=[jax.ShapeDtypeStruct((tokens, width), jnp.bfloat16)] * 2
        + [jax.ShapeDtypeStruct((slots * tokens, inner), jnp.bfloat16)] * 3
        + [jax.ShapeDtypeStruct((slots * tokens, width), jnp.bfloat16)] * 2,
        scratch_shapes=[
            pltpu.VMEM((3, width, inner), jnp.bfloat16),
            pltpu.SemaphoreType.DMA((len(parts),)),
        ],
        input_output_aliases={first + at: 2 + at for at in range(len(held))},
        compiler_params=pltpu.CompilerParams(vmem_limit_bytes=VMEM_BYTES),
        cost_estimate=cost(
            12 * tokens * width * inner, 2 * tokens * (4 * width + 3 * inner), tokens * inner
        ),
        name="feed",
    )(act, cot, *parts, *held)


def normalize_back(values, inverse, gain, upstream):
    weighted = upstream * gain
    inner = jnp.mean(weighted * values, -1, keepdims=True)
    value_grad = inverse * weighted - values * inverse * inverse * inverse * inner
    gain_grad = jnp.sum(upstream * values * inverse, 0)
    return (value_grad, gain_grad)


def inverse_of(values):
    return lax.rsqrt(jnp.mean(values * values, -1, keepdims=True) + EPS)


def rotary_tables():
    freq = BASE ** (-(jnp.arange(HD // 2, dtype=jnp.float32) * 2.0 / HD))
    angle = jnp.arange(SEQ_LEN, dtype=jnp.float32)[:, None] * freq[None, :]
    cosine, sine = jnp.cos(angle), jnp.sin(angle)
    cosine = jnp.concatenate([cosine] * 4, 1)
    sine = jnp.concatenate([-sine, sine, -sine, sine], 1)
    return cosine, sine


def body(
    sizes,
    block_input,
    first_gain,
    joint_weight,
    joint_bias,
    output_weight,
    second_gain,
    gate_weight,
    up_weight,
    down_weight,
    cotangent,
):
    grid = Grid(sizes)
    shard = gate_weight.shape[1]
    inner = -(-shard // LANES) * LANES
    wide = ((0, 0), (0, inner - shard))
    gain_size, bias_size = first_gain.shape[0], joint_bias.shape[0]
    stretch = (0, bias_size - gain_size)
    size = sizes["col"]
    small = jnp.stack([joint_bias, jnp.pad(first_gain, stretch), jnp.pad(second_gain, stretch)])
    small = grid.gather_small(small.astype(jnp.float32))
    weights = jnp.stack([gate_weight, up_weight, down_weight.T])
    weights = jnp.pad(weights, ((0, 0),) + wide)
    weight_half = half_of(weights, grid.odd_dp, 1)
    columns = after(jnp.concatenate([joint_weight, output_weight], 1), weight_half)
    ring_one = shift(weight_half, "row", sizes["row"])
    mine, last = grid.gather_columns(columns, {1: small, 3: ring_one})
    bias_full = small[0:1]
    first_scale, second_scale = (
        jnp.concatenate(
            [small[k : k + 1, j * bias_size : j * bias_size + gain_size] for j in range(size)], 1
        )
        for k in (1, 2)
    )
    other = flip(mine, "col", size, 1)
    joint_full, output_full = place_columns(mine, other, bias_size)
    cosine, sine = rotary_tables()
    cot_near = flip(cotangent, "col", size, 1)
    cot_far = flip(after(cotangent, last), "col", size, 2)

    first_act, joint = joint_projection(
        block_input, first_scale, joint_full, bias_full, cosine, sine
    )
    rows, pair = sizes["row"], sizes["dp"]
    ring_one = after(ring_one, last)
    rings = [ring_one, shift(ring_one, "row", rows)]
    turned = [flip(ring_one, "dp", pair, 1)]
    attended_low = attend(after(joint, (rings[1], turned[0])), 0, 4)
    rings[1] = after(rings[1], joint)
    rings.append(shift(rings[1], "row", rows))
    turned.append(flip(rings[1], "dp", pair, 1))
    attended_high = attend(after(joint, (rings[2], cot_far)), 4, 3)
    rings[2] = after(rings[2], attended_low)
    turned.append(flip(rings[2], "dp", pair, 1))
    parts = [weights]
    for ring, turn in zip(rings, turned):
        parts += [ring, turn]
    attended = after(jnp.concatenate([attended_low, attended_high], 1), turned)
    inputs = block_input.astype(jnp.float32)
    resid = inputs + dot(attended, output_full)
    second_inverse = inverse_of(resid)
    second_act = low(resid * second_inverse * second_scale)

    act_near = flip(second_act, "col", size, 1)
    act_far = flip(second_act, "col", size, 2)
    cot_last = flip(after(cot_far, attended_low), "col", size, 1)
    parts = [after(part, second_act) for part in parts]
    run = functools.partial(feed, (sizes["row"], sizes["dp"]))
    mix_own, grad_own, *held = run(0, size, second_act, cotangent, parts, ())
    cot_last = after(cot_last, grad_own)
    mix_near, grad_near, *held = run(1, size, act_near, cot_near, parts, held)
    act_far = after(act_far, grad_near)
    act_last = flip(act_far, "col", size, 1)
    mix_last, grad_last, *held = run(2, size, act_last, cot_last, parts, held)
    mix_far, grad_far, *held = run(3, size, act_far, cot_far, parts, held)
    hidden, gate_grad, up_grad, act_all, cot_all = held

    got_near = flip(grad_near, "col", size, 1)
    got_last = flip(grad_last, "col", size, 1)
    far_sum = add(grad_far, after(got_last, grad_far))
    got_far = flip(far_sum, "col", size, 2)

    down_part = low(dot(cot_all, after(hidden, far_sum), TN))
    down_mine = down_part.reshape(sizes["row"], -1, inner)
    down_got, sent = grid.ring_start(down_mine)
    gate_part = low(dot(act_all, after(gate_grad, sent), TN))
    gate_mine, gate_got, sent = grid.swap_halves(gate_part)
    down_total, down_got = grid.ring_step(down_mine, after(down_got, gate_part), 1)
    up_part = low(dot(act_all, after(up_grad, (sent, down_total)), TN))
    up_mine, up_got, sent = grid.swap_halves(up_part)
    got_far = after(got_far, sent)
    second_grad = grad_own.astype(jnp.float32) + got_near.astype(jnp.float32)
    second_grad = second_grad + got_far.astype(jnp.float32)
    resid_norm_grad, second_gain_grad = normalize_back(
        resid, second_inverse, second_scale, second_grad
    )
    resid_grad = cotangent.astype(jnp.float32) + resid_norm_grad
    proj_grad = low(resid_grad)
    attended_grad = low(dot(proj_grad, output_full, NT))
    mix_got = flip(after(mix_last, far_sum), "col", size, 1)
    mix_near = flip(after(mix_near, far_sum), "col", size, 1)
    mix_got = after(mix_got, attended_grad)
    mix_far = flip(add(mix_far, mix_got), "col", size, 2)
    output_part = low(dot(after(proj_grad, attended_grad), attended, TN))
    output_mine, output_got, sent = grid.core_parts(output_part)

    back = functools.partial(attend_back, joint)
    gate_mine = add(gate_mine, after(gate_got, proj_grad))
    gate_got, gate_sent = grid.ring_start(gate_mine)
    down_total, down_got = grid.ring_step(down_mine, after(down_got, proj_grad), 2)
    hold = after(attended_grad, (sent, down_total, gate_sent))
    query_low, *sums = back(hold, cosine, sine, 0, 3, ())

    down_total = grid.ring_step(down_mine, after(down_got, query_low), 3)
    down_got = flip(down_total, "dp", pair, 1)
    gate_total, gate_got = grid.ring_step(gate_mine, after(gate_got, query_low), 1)
    up_mine = add(up_mine, after(up_got, query_low))
    up_got, up_sent = grid.ring_start(up_mine)
    output_mine = add(output_mine, after(output_got, query_low))
    output_mine, output_got, sent = grid.pair_parts(output_mine)
    hold = after(attended_grad, (sent, gate_total, up_sent, down_total))
    query_mid, *sums = back(hold, cosine, sine, 3, 2, (query_low, *sums))

    gate_total, gate_got = grid.ring_step(gate_mine, after(gate_got, query_mid), 2)
    up_total, up_got = grid.ring_step(up_mine, after(up_got, query_mid), 1)
    down_w_grad = add(down_total, after(down_got, query_mid))
    hold = after(attended_grad, (up_total, gate_total, down_w_grad))
    joint_grad = back(hold, cosine, sine, 5, 2, (query_mid, *sums))[0]

    gate_total = grid.ring_step(gate_mine, after(gate_got, joint_grad), 3)
    up_total, up_got = grid.ring_step(up_mine, after(up_got, joint_grad), 2)
    joint_part = low(dot(after(joint_grad, (gate_total, up_total)), first_act, TN))
    gate_w_grad = grid.both_halves(gate_total)
    output_mine = add(output_mine, after(output_got, joint_grad))
    first_grad = dot(after(joint_grad, joint_part), joint_full, NT)
    bias_grad = jnp.sum(joint_grad.astype(jnp.float32), 0)
    first_inverse = inverse_of(inputs)
    input_norm_grad, first_gain_grad = normalize_back(
        inputs, first_inverse, first_scale, first_grad
    )
    input_grad = low(resid_grad + input_norm_grad)
    totals = jnp.concatenate([bias_grad, first_gain_grad, second_gain_grad])
    totals_got = grid.sum_axis(totals, "col")
    joint_mine, joint_got, _ = grid.core_parts(joint_part)
    joint_mine = add(joint_mine, joint_got)
    joint_mine, joint_got, sent = grid.pair_parts(joint_mine)
    up_total = grid.ring_step(up_mine, after(up_got, sent), 3)

    block_grad = jnp.concatenate([add(joint_mine, joint_got), output_mine], 0)
    half = block_grad.shape[0] // 2
    mine = half_of(block_grad, grid.odd_dp, 0)
    theirs = half_of(block_grad, 1 - grid.odd_dp, 0)
    got = flip(theirs, "dp", pair, 1)
    totals = sum(after(totals_got, theirs), totals)
    bit = 1
    while bit < rows:
        totals = totals + flip(totals, "row", rows, bit)
        bit *= 2
    mine = add(mine, got)
    up_w_grad = grid.both_halves(after(up_total, mine))
    totals = sum(grid.sum_axis(after(totals, mine), "dp"), totals)
    blocks = mine.reshape(half, rows, -1)
    block_grad = grid.both_halves(grid.scatter_direct(jnp.transpose(blocks, (1, 0, 2))))
    joint_w_grad, output_w_grad = block_grad[:bias_size].T, block_grad[bias_size:].T

    mix_far = after(mix_far, joint_grad).astype(jnp.float32)
    mixed = mix_own.astype(jnp.float32) + mix_near.astype(jnp.float32) + mix_far
    block_output = low(resid + mixed)

    def own(start, size):
        part = size // grid.col
        return lax.dynamic_slice_in_dim(totals, start + grid.at_col * part, part, 0)

    model = first_gain_grad.shape[0]
    wide_out = lambda values: values.astype(jnp.float32)
    return (
        block_output,
        input_grad,
        own(QKV, model),
        wide_out(joint_w_grad),
        own(0, QK_WIDTH),
        own(QK_WIDTH, KV_WIDTH),
        wide_out(output_w_grad),
        own(QKV + model, model),
        wide_out(gate_w_grad[:, :shard]),
        wide_out(up_w_grad[:, :shard]),
        wide_out(down_w_grad[:, :shard].T),
    )


def solution(mesh):
    tokens = P(("dp", "row", "col"), None)
    return jax.shard_map(
        functools.partial(body, dict(mesh.shape)),
        mesh=mesh,
        in_specs=(
            tokens,
            P("col"),
            P("row", "col"),
            P("col"),
            P("row", "col"),
            P("col"),
            P("row", "col"),
            P("row", "col"),
            P("col", "row"),
            tokens,
        ),
        out_specs=(
            tokens,
            tokens,
            P("col"),
            P("row", "col"),
            P("col"),
            P("col"),
            P("row", "col"),
            P("col"),
            P("row", "col"),
            P("row", "col"),
            P("col", "row"),
        ),
        check_vma=False,
    )
```

```python
import functools

import jax
import jax.numpy as jnp
from jax import lax
from jax.experimental import pallas as pl
from jax.experimental.pallas import tpu as pltpu
from jax.sharding import PartitionSpec as P

QH = 14
KVH = 2
HD = 64
SEQ_LEN = 1024
GROUP = QH // KVH
WIDTH = QH * HD
KV_WIDTH = KVH * HD
QK_WIDTH = WIDTH + KV_WIDTH
QKV = QK_WIDTH + KV_WIDTH

EPS = 1e-06
BASE = 1000000.0
MASKED = -1e30
LANES = 128
BLOCK = 256
FEED_BLOCK = 512

NN = (((1,), (0,)), ((), ()))
NT = (((1,), (1,)), ((), ()))
TN = (((0,), (0,)), ((), ()))
VMEM_BYTES = 56 * 1024 * 1024


def dot(left, right, dims=NN):
    return lax.dot_general(left, right, dims, preferred_element_type=jnp.float32)


def low(values):
    return values.astype(jnp.bfloat16)


def add(left, right):
    return low(left.astype(jnp.float32) + right.astype(jnp.float32))


def cost(flops, moved, transcendentals=0):
    return pl.CostEstimate(
        flops=int(flops) // 1000,
        bytes_accessed=int(moved) // 1000,
        transcendentals=int(transcendentals) // 1000,
    )


def flip(values, axis, size, bit):
    return lax.ppermute(values, axis, [(i, i ^ bit) for i in range(size)])


def shift(values, axis, size):
    return lax.ppermute(values, axis, [(i, (i + 1) % size) for i in range(size)])


def join(mine, other, odd, axis):
    first = jnp.where(odd, other, mine)
    second = jnp.where(odd, mine, other)
    return jnp.concatenate([first, second], axis)


def half_of(values, which, axis):
    size = values.shape[axis] // 2
    return lax.dynamic_slice_in_dim(values, which * size, size, axis)


def after(values, done):
    return lax.optimization_barrier((values, done))[0] if jax.tree.leaves(done) else values


class Grid:
    def __init__(self, sizes):
        self.dp, self.row, self.col = sizes["dp"], sizes["row"], sizes["col"]
        self.at_dp = lax.axis_index("dp")
        self.at_row = lax.axis_index("row")
        self.at_col = lax.axis_index("col")
        self.odd_dp = self.at_dp % 2
        self.core = self.at_col % 2
        self.pair = self.at_col // 2

    def gather_half_rows(self, block, axis):
        mine = half_of(block, self.odd_dp, axis)
        pairs = []
        for _ in range(1, self.row):
            mine = shift(mine, "row", self.row)
            pairs.append((mine, flip(mine, "dp", self.dp, 1)))
        return pairs, mine

    def gather_columns(self, block, at_step):
        other = flip(block, "col", self.col, 2)
        both = join(block[None], other[None], self.pair == 1, 0)
        size = both.shape[1]
        full = jnp.zeros((2, size * self.row, both.shape[2]), both.dtype)
        full = lax.dynamic_update_slice_in_dim(full, both, self.at_row * size, 1)
        mine = half_of(both, self.odd_dp, 1)
        for step in range(1, self.row):
            mine = shift(mine, "row", self.row)
            mine = at_step(step, mine)
            whole = join(mine, flip(mine, "dp", self.dp, 1), self.odd_dp == 1, 1)
            at = (self.at_row - step) % self.row
            full = lax.dynamic_update_slice_in_dim(full, whole, at * size, 1)
        return full, mine

    def gather_small(self, block):
        size = block.shape[1]
        both = join(block, flip(block, "col", self.col, 2), self.pair == 1, 1)
        other = flip(both, "col", self.col, 1)
        first = jnp.where(self.core == 1, other, both)
        second = jnp.where(self.core == 1, both, other)
        pieces = [first[:, :size], second[:, :size], first[:, size:], second[:, size:]]
        return jnp.concatenate(pieces, 1)

    def swap_halves(self, part):
        size = part.shape[0] // self.row
        blocks = part.reshape(self.row, size, part.shape[1])
        mine = half_of(blocks, self.odd_dp, 1)
        theirs = half_of(blocks, 1 - self.odd_dp, 1)
        return mine, flip(theirs, "dp", self.dp, 1), theirs

    def sum_pairs(self, total):
        bit = 2
        while bit < self.dp:
            total = add(total, flip(total, "dp", self.dp, bit))
            bit *= 2
        return total

    def own_block(self, mine, step):
        at = (self.at_row - step) % self.row
        return lax.dynamic_index_in_dim(mine, at, 0, False)

    def ring_start(self, mine):
        sent = self.own_block(mine, 1)
        return shift(sent, "row", self.row), sent

    def ring_step(self, mine, got, step):
        total = add(got, self.own_block(mine, step + 1))
        if step < self.row - 1:
            return total, shift(total, "row", self.row)
        return self.sum_pairs(total)

    def scatter_direct(self, mine):
        total = lax.dynamic_index_in_dim(mine, self.at_row, 0, False).astype(jnp.float32)
        for step in range(1, self.row):
            to = (self.at_row + step) % self.row
            block = lax.dynamic_index_in_dim(mine, to, 0, False)
            pairs = [(i, (i + step) % self.row) for i in range(self.row)]
            total = total + lax.ppermute(block, "row", pairs).astype(jnp.float32)
        return self.sum_pairs(low(total))

    def sum_axis(self, values, axis):
        size = getattr(self, axis)
        return [
            lax.ppermute(values, axis, [(i, (i + step) % size) for i in range(size)])
            for step in range(1, size)
        ]

    def both_halves(self, total):
        other = flip(total, "dp", self.dp, 1)
        return join(total, other, self.odd_dp == 1, 0)

    def core_parts(self, part):
        size = part.shape[0] // self.col
        pieces = part.reshape(self.col, size, part.shape[1])
        evens, odds = jnp.stack([pieces[0], pieces[2]]), jnp.stack([pieces[1], pieces[3]])
        mine = jnp.where(self.core == 1, odds, evens)
        theirs = jnp.where(self.core == 1, evens, odds)
        return mine, flip(theirs, "col", self.col, 1), theirs

    def pair_parts(self, both):
        mine = jnp.where(self.pair == 1, both[1], both[0])
        theirs = jnp.where(self.pair == 1, both[0], both[1])
        return mine, flip(theirs, "col", self.col, 2), theirs


def turn_pairs(values, cosine, sine):
    lane = lax.broadcasted_iota(jnp.int32, values.shape, 1)
    before = pltpu.roll(values, HD // 2, 1)
    after = pltpu.roll(values, LANES - HD // 2, 1)
    partner = jnp.where(lane % HD < HD // 2, after, before)
    return values * cosine + partner * sine


def place_kernel(joint_size, mine_ref, other_ref, joint_ref, output_ref):
    core = lax.axis_index("col") % 2
    size = mine_ref.shape[2]
    rest = size - joint_size

    def place(first_ref, second_ref):
        pieces = (first_ref[0], second_ref[0], first_ref[1], second_ref[1])
        for j, piece in enumerate(pieces):
            joint_ref[:, j * joint_size : (j + 1) * joint_size] = piece[:, :joint_size]
            output_ref[:, j * rest : (j + 1) * rest] = piece[:, joint_size:]

    @pl.when(core == 0)
    def _():
        place(mine_ref, other_ref)

    @pl.when(core == 1)
    def _():
        place(other_ref, mine_ref)


def place_columns(mine, other, joint_size):
    _, rows, size = mine.shape
    step = rows // 4
    block = pl.BlockSpec((2, step, size), lambda i: (0, i, 0))
    widths = (4 * joint_size, 4 * (size - joint_size))
    return pl.pallas_call(
        functools.partial(place_kernel, joint_size),
        grid=(4,),
        in_specs=[block, block],
        out_specs=[pl.BlockSpec((step, width), lambda i: (i, 0)) for width in widths],
        out_shape=[jax.ShapeDtypeStruct((rows, width), jnp.bfloat16) for width in widths],
        compiler_params=pltpu.CompilerParams(vmem_limit_bytes=VMEM_BYTES),
        cost_estimate=cost(0, 16 * rows * size),
        name="place_columns",
    )(mine, other)


def joint_kernel(x_ref, gain_ref, weight_ref, bias_ref, cos_ref, sin_ref, act_ref, out_ref):
    inputs = x_ref[...].astype(jnp.float32)
    inverse = lax.rsqrt(jnp.mean(inputs * inputs, -1, keepdims=True) + EPS)
    act = low(inputs * inverse * gain_ref[...])
    act_ref[...] = act
    joint = dot(act, weight_ref[...]) + bias_ref[...]
    cosine, sine = cos_ref[...], sin_ref[...]
    for start in range(0, QK_WIDTH, LANES):
        turned = turn_pairs(joint[:, start : start + LANES], cosine, sine)
        out_ref[:, start : start + LANES] = low(turned)
    out_ref[:, QK_WIDTH:] = low(joint[:, QK_WIDTH:])


def joint_projection(inputs, gain, weight, bias, cosine, sine):
    tokens, width = inputs.shape
    steps = SEQ_LEN // BLOCK
    return pl.pallas_call(
        joint_kernel,
        grid=(tokens // BLOCK,),
        in_specs=[
            pl.BlockSpec((BLOCK, width), lambda i: (i, 0)),
            pl.BlockSpec((1, width), lambda i: (0, 0)),
            pl.BlockSpec((width, QKV), lambda i: (0, 0)),
            pl.BlockSpec((1, QKV), lambda i: (0, 0)),
            pl.BlockSpec((BLOCK, LANES), lambda i: (i % steps, 0)),
            pl.BlockSpec((BLOCK, LANES), lambda i: (i % steps, 0)),
        ],
        out_specs=[
            pl.BlockSpec((BLOCK, width), lambda i: (i, 0)),
            pl.BlockSpec((BLOCK, QKV), lambda i: (i, 0)),
        ],
        out_shape=[
            jax.ShapeDtypeStruct((tokens, width), jnp.bfloat16),
            jax.ShapeDtypeStruct((tokens, QKV), jnp.bfloat16),
        ],
        compiler_params=pltpu.CompilerParams(vmem_limit_bytes=VMEM_BYTES),
        cost_estimate=cost(2 * tokens * width * QKV * 2, 8 * tokens * QKV),
        name="joint_projection",
    )(inputs, gain, weight, bias, cosine, sine)


def select_head(values, head):
    return jnp.where(head // GROUP == 0, values[:, :HD], values[:, HD:])


def mask_last(scores, start, key_axis):
    square = (BLOCK, BLOCK)
    keys_at = lax.broadcasted_iota(jnp.int32, square, key_axis)
    rows_at = lax.broadcasted_iota(jnp.int32, square, 1 - key_axis)
    last = lax.slice_in_dim(scores, start, start + BLOCK, axis=key_axis)
    last = jnp.where(keys_at <= rows_at, last, MASKED)
    if start == 0:
        return last
    return jnp.concatenate([lax.slice_in_dim(scores, 0, start, axis=key_axis), last], key_axis)


def attend_kernel(first, q_ref, k_ref, v_ref, out_ref):
    pair = pl.program_id(1) + first
    scale = HD ** (-0.5)
    lanes = [slice(e * HD, (e + 1) * HD) for e in range(2)]
    keys = [select_head(k_ref[...], 2 * pair + e) for e in range(2)]
    values = [select_head(v_ref[...], 2 * pair + e) for e in range(2)]
    values = [jnp.concatenate([item, jnp.ones_like(item)], 1) for item in values]
    for group in ((3, 2, 1, 0),):
        jobs = [(i, e) for i in group for e in range(2)]
        query = [q_ref[i * BLOCK : (i + 1) * BLOCK, lanes[e]] * jnp.bfloat16(scale) for i, e in jobs]
        scores = [dot(a, keys[e][: (i + 1) * BLOCK], NT) for a, (i, e) in zip(query, jobs)]
        scores = [mask_last(item, i * BLOCK, 1) for item, (i, e) in zip(scores, jobs)]
        weights = [jnp.exp(item - jnp.max(item, -1, keepdims=True)) for item in scores]
        both = [dot(low(a), values[e][: (i + 1) * BLOCK]) for a, (i, e) in zip(weights, jobs)]
        attended = [item[:, :HD] / item[:, HD : HD + 1] for item in both]
        for at, i in enumerate(group):
            both_heads = jnp.concatenate(attended[2 * at : 2 * at + 2], 1)
            out_ref[i * BLOCK : (i + 1) * BLOCK, :] = low(both_heads)


def attend(joint, first, pairs):
    tokens = joint.shape[0]
    seqs = tokens // SEQ_LEN
    return pl.pallas_call(
        functools.partial(attend_kernel, first),
        grid=(seqs, pairs),
        in_specs=[
            pl.BlockSpec((SEQ_LEN, LANES), lambda s, p: (s, p + first)),
            pl.BlockSpec((SEQ_LEN, LANES), lambda s, p: (s, WIDTH // LANES)),
            pl.BlockSpec((SEQ_LEN, LANES), lambda s, p: (s, QK_WIDTH // LANES)),
        ],
        out_specs=pl.BlockSpec((SEQ_LEN, LANES), lambda s, p: (s, p)),
        out_shape=jax.ShapeDtypeStruct((tokens, pairs * LANES), jnp.bfloat16),
        compiler_params=pltpu.CompilerParams(vmem_limit_bytes=VMEM_BYTES),
        cost_estimate=cost(
            tokens * SEQ_LEN * pairs * 1024, 8 * tokens * pairs * LANES, tokens * 1024 * pairs
        ),
        name="attend",
    )(joint, joint, joint)


def attend_back_kernel(first, last, *refs):
    q_ref, k_ref, v_ref, g_ref, cos_ref, sin_ref = refs[:6]
    if first > 0:
        key_in, value_in = refs[7:9]
    ends = last == QH // 2 - 1
    if not ends:
        dk_ref, dv_ref = refs[-4:-2]
    dq_ref = refs[-3] if ends else refs[-5]
    key_sum, value_sum = refs[-2:]
    pair = pl.program_id(1) + first
    scale = HD ** (-0.5)

    @pl.when(pair == first)
    def _():
        key_sum[...] = key_in[...] if first > 0 else jnp.zeros_like(key_sum)
        value_sum[...] = value_in[...] if first > 0 else jnp.zeros_like(value_sum)

    @pl.when(pair <= last)
    def _():
        heads = [2 * pair + e for e in range(2)]
        lanes = [slice(e * HD, (e + 1) * HD) for e in range(2)]
        all_keys = [select_head(k_ref[...], head) for head in heads]
        all_values = [select_head(v_ref[...], head) for head in heads]
        for group in ((3,), (0, 1, 2)):
            jobs = [(i, e) for i in group for e in range(2)]
            keys = [all_keys[e][: (i + 1) * BLOCK] for i, e in jobs]
            values = [all_values[e][: (i + 1) * BLOCK] for i, e in jobs]
            spans = [slice(i * BLOCK, (i + 1) * BLOCK) for i, e in jobs]
            query = [
                q_ref[span, lanes[e]] * jnp.bfloat16(scale) for span, (i, e) in zip(spans, jobs)
            ]
            grad = [g_ref[span, lanes[e]] for span, (i, e) in zip(spans, jobs)]
            scores = [dot(a, b, NT) for a, b in zip(keys, query)]
            prob_grad = [dot(a, b, NT) for a, b in zip(values, grad)]
            scores = [mask_last(item, i * BLOCK, 0) for item, (i, e) in zip(scores, jobs)]
            weights = [jnp.exp(item - jnp.max(item, 0, keepdims=True)) for item in scores]
            prob = [item * (1.0 / jnp.sum(item, 0, keepdims=True)) for item in weights]
            inner = [jnp.sum(a * b, 0, keepdims=True) for a, b in zip(prob, prob_grad)]
            score_grad = [low(a * (b - c)) for a, b, c in zip(prob, prob_grad, inner)]
            value_grad = [dot(low(a), b) for a, b in zip(prob, grad)]
            key_grad = [dot(a, b) for a, b in zip(score_grad, query)]
            parts = [dot(a, b, TN) for a, b in zip(keys, score_grad)]
            for (i, e), value_part, key_part in zip(jobs, value_grad, key_grad):
                value_sum[heads[e] // GROUP, : (i + 1) * BLOCK, :] += value_part
                key_sum[heads[e] // GROUP, : (i + 1) * BLOCK, :] += key_part
            for at, i in enumerate(group):
                rows = pl.ds(i * BLOCK, BLOCK)
                query_grad = jnp.transpose(jnp.concatenate(parts[2 * at : 2 * at + 2], 0)) * scale
                turned = turn_pairs(query_grad, cos_ref[rows, :], -sin_ref[rows, :])
                dq_ref[rows, :] = low(turned)

    if not ends:

        @pl.when(pair == last)
        def _():
            dk_ref[...] = key_sum[...]
            dv_ref[...] = value_sum[...]

        return

    @pl.when(pair == last + 1)
    def _():
        key_grad = jnp.concatenate([key_sum[0], key_sum[1]], 1)
        dq_ref[...] = low(turn_pairs(key_grad, cos_ref[...], -sin_ref[...]))

    @pl.when(pair == last + 2)
    def _():
        dq_ref[...] = low(jnp.concatenate([value_sum[0], value_sum[1]], 1))


def attend_back(joint, grad, cosine, sine, first, pairs, sums):
    tokens = joint.shape[0]
    last = first + pairs - 1
    ends = last == QH // 2 - 1
    seqs = tokens // SEQ_LEN
    steps = pairs + 2 if ends else pairs
    block = (SEQ_LEN, LANES)
    held = pl.BlockSpec((KVH, SEQ_LEN, HD), lambda s, p: (s, 0, 0))
    return pl.pallas_call(
        functools.partial(attend_back_kernel, first, last),
        grid=(seqs, steps),
        in_specs=[
            pl.BlockSpec(block, lambda s, p: (s, jnp.minimum(p + first, last))),
            pl.BlockSpec(block, lambda s, p: (s, WIDTH // LANES)),
            pl.BlockSpec(block, lambda s, p: (s, QK_WIDTH // LANES)),
            pl.BlockSpec(block, lambda s, p: (s, jnp.minimum(p + first, last))),
            pl.BlockSpec(block, lambda s, p: (0, 0)),
            pl.BlockSpec(block, lambda s, p: (0, 0)),
        ]
        + ([pl.BlockSpec(memory_space=pl.ANY), held, held] if sums else []),
        out_specs=[pl.BlockSpec(block, lambda s, p: (s, p + first))]
        + ([] if ends else [held] * 2),
        out_shape=[jax.ShapeDtypeStruct((tokens, QKV), jnp.bfloat16)]
        + [jax.ShapeDtypeStruct((seqs * KVH, SEQ_LEN, HD), jnp.float32)] * (0 if ends else 2),
        input_output_aliases={6: 0} if sums else {},
        scratch_shapes=[
            pltpu.VMEM((KVH, SEQ_LEN, HD), jnp.float32),
            pltpu.VMEM((KVH, SEQ_LEN, HD), jnp.float32),
        ],
        compiler_params=pltpu.CompilerParams(vmem_limit_bytes=VMEM_BYTES),
        cost_estimate=cost(
            tokens * SEQ_LEN * pairs * 2560, 8 * tokens * pairs * LANES, tokens * 1024 * pairs
        ),
        name="attend_back",
    )(joint, joint, joint, grad, cosine, sine, *sums)


def feed_kernel(sizes, held, *refs):
    rows, dps = sizes
    pieces = 2 * rows - 1
    act_ref, cot_ref = refs[:2]
    parts = refs[2 : 2 + pieces]
    outs = refs[2 + pieces + held :]
    mix_ref, grad_ref, hid_ref, dgate_ref, dup_ref, act_out, cot_out, weight_ref, sems = outs
    size = parts[0].shape[1]
    half = size // 2

    @pl.when(pl.program_id(0) == 0)
    def _():
        row, odd = lax.axis_index("row"), lax.axis_index("dp") % 2
        copies = []
        for at, part in enumerate(parts):
            step = (at + 1) // 2
            start = (row + rows - step) % rows * size
            if at > 0:
                start = start + half * (odd if at % 2 == 1 else 1 - odd)
            span = pl.ds(pl.multiple_of(start, 16), part.shape[1])
            copies.append(pltpu.make_async_copy(part, weight_ref.at[:, span, :], sems.at[at]))
        for copy in copies:
            copy.start()
        for copy in copies:
            copy.wait()

    act, cot = act_ref[...], cot_ref[...]
    act_out[...] = act
    cot_out[...] = cot
    gate_ref, up_ref, down_ref = weight_ref.at[0], weight_ref.at[1], weight_ref.at[2]
    gate = dot(act, gate_ref[...])
    up_part = dot(act, up_ref[...])
    hidden_grad = dot(cot, down_ref[...])
    sigma = jax.nn.sigmoid(gate)
    silu = gate * sigma
    hidden = low(silu * up_part)
    gate_grad = low(hidden_grad * up_part * sigma * (1.0 + gate * (1.0 - sigma)))
    up_grad = low(hidden_grad * silu)
    hid_ref[...] = hidden
    dgate_ref[...] = gate_grad
    dup_ref[...] = up_grad
    mix_ref[...] = low(dot(hidden, down_ref[...], NT))
    grad_ref[...] = low(dot(gate_grad, gate_ref[...], NT) + dot(up_grad, up_ref[...], NT))


def feed(sizes, slot, slots, act, cot, parts, held):
    tokens, width = act.shape
    inner = parts[0].shape[2]
    steps = tokens // FEED_BLOCK
    narrow = pl.BlockSpec((FEED_BLOCK, width), lambda i: (i, 0))
    narrow_at = pl.BlockSpec((FEED_BLOCK, width), lambda i: (i + slot * steps, 0))
    wide_at = pl.BlockSpec((FEED_BLOCK, inner), lambda i: (i + slot * steps, 0))
    anywhere = pl.BlockSpec(memory_space=pl.ANY)
    first = 2 + len(parts)
    return pl.pallas_call(
        functools.partial(feed_kernel, sizes, len(held)),
        grid=(steps,),
        in_specs=[narrow, narrow] + [anywhere] * (len(parts) + len(held)),
        out_specs=[narrow, narrow, wide_at, wide_at, wide_at, narrow_at, narrow_at],
        out_shape=[jax.ShapeDtypeStruct((tokens, width), jnp.bfloat16)] * 2
        + [jax.ShapeDtypeStruct((slots * tokens, inner), jnp.bfloat16)] * 3
        + [jax.ShapeDtypeStruct((slots * tokens, width), jnp.bfloat16)] * 2,
        scratch_shapes=[
            pltpu.VMEM((3, width, inner), jnp.bfloat16),
            pltpu.SemaphoreType.DMA((len(parts),)),
        ],
        input_output_aliases={first + at: 2 + at for at in range(len(held))},
        compiler_params=pltpu.CompilerParams(vmem_limit_bytes=VMEM_BYTES),
        cost_estimate=cost(
            12 * tokens * width * inner, 2 * tokens * (4 * width + 3 * inner), tokens * inner
        ),
        name="feed",
    )(act, cot, *parts, *held)


def normalize_back(values, inverse, gain, upstream):
    weighted = upstream * gain
    inner = jnp.mean(weighted * values, -1, keepdims=True)
    value_grad = inverse * weighted - values * inverse * inverse * inverse * inner
    gain_grad = jnp.sum(upstream * values * inverse, 0)
    return (value_grad, gain_grad)


def inverse_of(values):
    return lax.rsqrt(jnp.mean(values * values, -1, keepdims=True) + EPS)


def rotary_tables():
    freq = BASE ** (-(jnp.arange(HD // 2, dtype=jnp.float32) * 2.0 / HD))
    angle = jnp.arange(SEQ_LEN, dtype=jnp.float32)[:, None] * freq[None, :]
    cosine, sine = jnp.cos(angle), jnp.sin(angle)
    cosine = jnp.concatenate([cosine] * 4, 1)
    sine = jnp.concatenate([-sine, sine, -sine, sine], 1)
    return cosine, sine


def body(
    sizes,
    block_input,
    first_gain,
    joint_weight,
    joint_bias,
    output_weight,
    second_gain,
    gate_weight,
    up_weight,
    down_weight,
    cotangent,
):
    grid = Grid(sizes)
    shard = gate_weight.shape[1]
    inner = -(-shard // LANES) * LANES
    wide = ((0, 0), (0, inner - shard))
    gain_size, bias_size = first_gain.shape[0], joint_bias.shape[0]
    stretch = (0, bias_size - gain_size)
    size = sizes["col"]
    weights = jnp.stack([gate_weight, up_weight, down_weight.T])
    weights = jnp.pad(weights, ((0, 0),) + wide)
    weight_half = half_of(weights, grid.odd_dp, 1)
    small = jnp.stack([joint_bias, jnp.pad(first_gain, stretch), jnp.pad(second_gain, stretch)])
    small = grid.gather_small(after(small.astype(jnp.float32), weight_half))
    cosine, sine = rotary_tables()
    columns = after(jnp.concatenate([joint_weight, output_weight], 1), weight_half)
    rows, pair = sizes["row"], sizes["dp"]
    rings = [shift(weight_half, "row", rows)]
    turned = []

    def at_step(step, mine):
        if step == 1:
            mine = after(mine, small)
            rings[0] = after(rings[0], mine)
            rings.append(shift(rings[0], "row", rows))
            turned.append(flip(rings[0], "dp", pair, 1))
        elif step == 2:
            mine = after(mine, (cosine, sine, rings[1], turned[0]))
        return mine

    mine, last = grid.gather_columns(columns, at_step)
    rings[1] = after(rings[1], last)
    turned.append(flip(rings[1], "dp", pair, 1))
    rings.append(shift(rings[1], "row", rows))
    bias_full = small[0:1]
    first_scale, second_scale = (
        jnp.concatenate(
            [small[k : k + 1, j * bias_size : j * bias_size + gain_size] for j in range(size)], 1
        )
        for k in (1, 2)
    )
    other = flip(mine, "col", size, 1)
    joint_full, output_full = place_columns(mine, other, bias_size)
    cot_near = flip(cotangent, "col", size, 1)
    cot_far = flip(after(cotangent, last), "col", size, 2)

    first_act, joint = joint_projection(
        block_input, first_scale, joint_full, bias_full, cosine, sine
    )
    attended = attend(after(joint, (rings[2], turned[1])), 0, QH // 2)
    rings[2] = after(rings[2], joint)
    turned.append(flip(rings[2], "dp", pair, 1))
    parts = [weights]
    for ring, turn in zip(rings, turned):
        parts += [ring, turn]
    attended = after(attended, (turned[2], cot_far))
    inputs = block_input.astype(jnp.float32)
    resid = inputs + dot(attended, output_full)
    second_inverse = inverse_of(resid)
    second_act = low(resid * second_inverse * second_scale)

    act_near = flip(second_act, "col", size, 1)
    act_far = flip(second_act, "col", size, 2)
    cot_last = flip(after(cot_far, attended), "col", size, 1)
    parts = [after(part, second_act) for part in parts]
    run = functools.partial(feed, (sizes["row"], sizes["dp"]))
    mix_own, grad_own, *held = run(0, size, second_act, cotangent, parts, ())
    cot_last = after(cot_last, grad_own)
    mix_near, grad_near, *held = run(1, size, act_near, cot_near, parts, held)
    act_far = after(act_far, grad_near)
    act_last = flip(act_far, "col", size, 1)
    mix_last, grad_last, *held = run(2, size, act_last, cot_last, parts, held)
    mix_far, grad_far, *held = run(3, size, act_far, cot_far, parts, held)
    hidden, gate_grad, up_grad, act_all, cot_all = held

    got_near = flip(grad_near, "col", size, 1)
    got_last = flip(grad_last, "col", size, 1)
    far_sum = add(grad_far, after(got_last, grad_far))
    got_far = flip(far_sum, "col", size, 2)

    down_part = low(dot(cot_all, after(hidden, far_sum), TN))
    down_mine = down_part.reshape(sizes["row"], -1, inner)
    down_got, sent = grid.ring_start(down_mine)
    gate_part = low(dot(act_all, after(gate_grad, sent), TN))
    gate_mine, gate_got, sent = grid.swap_halves(gate_part)
    down_total, down_got = grid.ring_step(down_mine, after(down_got, gate_part), 1)
    up_part = low(dot(act_all, after(up_grad, (sent, down_total)), TN))
    up_mine, up_got, sent = grid.swap_halves(up_part)
    got_far = after(got_far, sent)
    second_grad = grad_own.astype(jnp.float32) + got_near.astype(jnp.float32)
    second_grad = second_grad + got_far.astype(jnp.float32)
    resid_norm_grad, second_gain_grad = normalize_back(
        resid, second_inverse, second_scale, second_grad
    )
    resid_grad = cotangent.astype(jnp.float32) + resid_norm_grad
    proj_grad = low(resid_grad)
    attended_grad = low(dot(proj_grad, output_full, NT))
    mix_got = flip(after(mix_last, far_sum), "col", size, 1)
    mix_near = flip(after(mix_near, far_sum), "col", size, 1)
    mix_got = after(mix_got, attended_grad)
    mix_far = flip(add(mix_far, mix_got), "col", size, 2)
    output_part = low(dot(after(proj_grad, attended_grad), attended, TN))
    output_mine, output_got, sent = grid.core_parts(output_part)

    back = functools.partial(attend_back, joint)
    gate_mine = add(gate_mine, after(gate_got, proj_grad))
    gate_got, gate_sent = grid.ring_start(gate_mine)
    down_total, down_got = grid.ring_step(down_mine, after(down_got, proj_grad), 2)
    hold = after(attended_grad, (sent, down_total, gate_sent))
    query_low, *sums = back(hold, cosine, sine, 0, 3, ())

    down_total = grid.ring_step(down_mine, after(down_got, query_low), 3)
    down_got = flip(down_total, "dp", pair, 1)
    gate_total, gate_got = grid.ring_step(gate_mine, after(gate_got, query_low), 1)
    up_mine = add(up_mine, after(up_got, query_low))
    up_got, up_sent = grid.ring_start(up_mine)
    output_mine = add(output_mine, after(output_got, query_low))
    output_mine, output_got, sent = grid.pair_parts(output_mine)
    hold = after(attended_grad, (sent, gate_total, up_sent, down_total))
    query_mid, *sums = back(hold, cosine, sine, 3, 2, (query_low, *sums))

    gate_total, gate_got = grid.ring_step(gate_mine, after(gate_got, query_mid), 2)
    up_total, up_got = grid.ring_step(up_mine, after(up_got, query_mid), 1)
    down_w_grad = add(down_total, after(down_got, query_mid))
    hold = after(attended_grad, (up_total, gate_total, down_w_grad))
    joint_grad = back(hold, cosine, sine, 5, 2, (query_mid, *sums))[0]

    gate_total = grid.ring_step(gate_mine, after(gate_got, joint_grad), 3)
    up_total, up_got = grid.ring_step(up_mine, after(up_got, joint_grad), 2)
    joint_part = low(dot(after(joint_grad, (gate_total, up_total)), first_act, TN))
    gate_w_grad = grid.both_halves(gate_total)
    output_mine = add(output_mine, after(output_got, joint_grad))
    output_half = half_of(output_mine, grid.odd_dp, 0)
    output_got = flip(half_of(output_mine, 1 - grid.odd_dp, 0), "dp", pair, 1)
    first_grad = dot(after(joint_grad, joint_part), joint_full, NT)
    bias_grad = jnp.sum(joint_grad.astype(jnp.float32), 0)
    first_inverse = inverse_of(inputs)
    input_norm_grad, first_gain_grad = normalize_back(
        inputs, first_inverse, first_scale, first_grad
    )
    input_grad = low(resid_grad + input_norm_grad)
    totals = jnp.concatenate([bias_grad, first_gain_grad, second_gain_grad])
    totals_got = grid.sum_axis(totals, "col")
    joint_mine, joint_got, _ = grid.core_parts(joint_part)
    joint_mine = add(joint_mine, joint_got)
    joint_mine, joint_got, sent = grid.pair_parts(joint_mine)
    up_total = grid.ring_step(up_mine, after(up_got, sent), 3)

    joint_mine = add(joint_mine, joint_got)
    half = bias_size // 2
    mine = half_of(joint_mine, grid.odd_dp, 0)
    theirs = half_of(joint_mine, 1 - grid.odd_dp, 0)
    got = flip(theirs, "dp", pair, 1)
    totals = sum(after(totals_got, theirs), totals)
    bit = 1
    while bit < rows:
        totals = totals + flip(totals, "row", rows, bit)
        bit *= 2
    output_half = add(output_half, after(output_got, sent))
    mine = jnp.concatenate([add(mine, got), output_half], 0)
    up_w_grad = grid.both_halves(after(up_total, mine))
    totals = sum(grid.sum_axis(after(totals, mine), "dp"), totals)
    blocks = mine.reshape(mine.shape[0], rows, -1)
    total = grid.scatter_direct(jnp.transpose(blocks, (1, 0, 2)))
    other = flip(total, "dp", pair, 1)
    joint_w_grad, output_w_grad = (
        join(total[at], other[at], grid.odd_dp == 1, 0).T
        for at in (slice(0, half), slice(half, None))
    )

    mix_far = after(mix_far, joint_grad).astype(jnp.float32)
    mixed = mix_own.astype(jnp.float32) + mix_near.astype(jnp.float32) + mix_far
    block_output = low(resid + mixed)

    def own(start, size):
        part = size // grid.col
        return lax.dynamic_slice_in_dim(totals, start + grid.at_col * part, part, 0)

    model = first_gain_grad.shape[0]
    wide_out = lambda values: values.astype(jnp.float32)
    return (
        block_output,
        input_grad,
        own(QKV, model),
        wide_out(joint_w_grad),
        own(0, QK_WIDTH),
        own(QK_WIDTH, KV_WIDTH),
        wide_out(output_w_grad),
        own(QKV + model, model),
        wide_out(gate_w_grad[:, :shard]),
        wide_out(up_w_grad[:, :shard]),
        wide_out(down_w_grad[:, :shard].T),
    )


def solution(mesh):
    tokens = P(("dp", "row", "col"), None)
    return jax.shard_map(
        functools.partial(body, dict(mesh.shape)),
        mesh=mesh,
        in_specs=(
            tokens,
            P("col"),
            P("row", "col"),
            P("col"),
            P("row", "col"),
            P("col"),
            P("row", "col"),
            P("row", "col"),
            P("col", "row"),
            tokens,
        ),
        out_specs=(
            tokens,
            tokens,
            P("col"),
            P("row", "col"),
            P("col"),
            P("col"),
            P("row", "col"),
            P("col"),
            P("row", "col"),
            P("row", "col"),
            P("col", "row"),
        ),
        check_vma=False,
    )
```
